512 devices in a mesh: dp: 8 (over z), tensor: 8 (over y), factor: 8 (over x, core).
Axes of the slice: x: 4, y: 8, z: 8, core: 2. Of those that a mesh axis runs over, the one named last changes fastest.
Arguments:
- resid: bfloat16 [4096, 8192], P('dp', ('tensor', 'factor')), may hold values from -60 to 60
- norm_gain: bfloat16 [8192], P(('tensor', 'factor')), may hold values from 0.5 to 1.5
- cotangent: bfloat16 [4096, 2, 64], P('dp'), may hold values from -0.059814453 to 0.059814453
- segment_ids: int32 [8, 512], P('dp'), may hold values from 0 to 1, never falling along the last dimension, each value on 1 to 511 neighbouring positions
- query_grads: bfloat16 [16, 2, 64, 8192], P('dp', None, None, ('tensor', 'factor')), may hold values from -0.011962891 to 0.011962891
- input_basis: bfloat16 [2, 8192, 8192], P(None, 'tensor', ('dp', 'factor')), may hold values from -0.0625 to 0.0625
- output_basis: bfloat16 [2, 64, 64], replicated, may hold values from -0.75 to 0.75
- eigenvalues: float32 [2, 64, 8192], P(None, None, ('dp', 'factor')), may hold values from 0.003 to 3
Outputs:
- scores: float32 [16, 16], replicated
The draws below stay inside these ranges and needn't reach their ends.
Inputs may be any that keep to these rules, and one draw needn't show every extreme that they name: `segment_ids`: in each row ids never fall and every id appears; a candidate has at most 511 tokens.
All inputs are finite; a program needn't handle non-finite values.
Results may differ from the reference program's by a relative error of at most 0.005.
Values may be sent and summed in bfloat16 or wider, within the bound.
No kernel may reach another device: no remote copies, remote signals or barrier semaphores. Data moves between devices by JAX's collectives and lax.ppermute only.
A program may use at most 64 MiB of HBM per device.

```python
import math
import jax
import jax.numpy as jnp
import numpy as np
from jax import lax

D = 8192
R = 64
TOK_DEV = 512
CAND_DEV = 2
TOKENS = 4096
CANDS = 16
NQ = 16
N_DP = 8


def draw_resid(key, part):
    key = jax.random.fold_in(key, 11)
    first = jax.random.fold_in(key, 0)
    base = jnp.clip(jax.random.normal(first, (TOKENS, D), jnp.float32), -6.0, 6.0)
    rising = jnp.exp(jnp.log(3.0) * jnp.arange(D, dtype=jnp.float32) / D)
    return (base * rising).astype(jnp.bfloat16)


def draw_eigenvalues(key, part):
    key = jax.random.fold_in(key, 23)
    uniform_part = jax.random.uniform(key, (2, R, D), jnp.float32)
    rising = jnp.exp(jnp.log(3.0) * jnp.arange(D, dtype=jnp.float32) / D)
    lowest = jnp.log(0.01)
    return jnp.exp(lowest - lowest * uniform_part) * rising


def block_levels(key, extent, pieces, least, high):
    def one(position, parts):
        draws = jax.random.uniform(jax.random.fold_in(jax.random.fold_in(key, 6), position), (parts,), jnp.float32, least / len(pieces), high / len(pieces))
        return jnp.repeat(jnp.exp(draws), extent[position] // parts).reshape((-1,) + (1,) * (len(extent) - position - 1))

    level = one(*pieces[0])
    for cut in pieces[1:]:
        level = level * one(*cut)
    return level


def profile(number_of, total, reach, slope):
    weights = [(1 << 20) // math.isqrt(standing ** slope) + 1 for standing in range(2, number_of + 1)]
    surplus, holding = total - reach - (number_of - 1), [1] * (number_of - 1)
    while surplus > 0:
        movable = [i for i in range(number_of - 1) if holding[i] < reach]
        mass, remaining = sum([weights[i] for i in movable]), surplus
        for i in movable:
            extra = min(reach - holding[i], max(1, remaining * weights[i] // mass), surplus)
            holding[i] = holding[i] + extra
            surplus = surplus - extra
    return np.array([reach] + holding)


def ragged(stream_key, amount, total, reach, slope):
    if amount == 2:
        one = jax.random.randint(stream_key, (), max(1, total - reach), min(reach, total - 1) + 1)
        return jnp.stack([one, total - one])
    tallies = jnp.asarray(profile(amount, total, reach, slope), jnp.int32)
    couples = (amount - 1) // 2
    donor, taker = tallies[1:1 + 2 * couples:2], tallies[2:2 + 2 * couples:2]
    room = jnp.minimum(donor - 1, reach - taker)
    passed = jax.random.randint(jax.random.fold_in(stream_key, 1), (couples,), 0, 1 << 20) % (room + 1)
    tallies = tallies.at[1:1 + 2 * couples:2].set(donor - passed).at[2:2 + 2 * couples:2].set(taker + passed)
    return tallies[jax.random.permutation(jax.random.fold_in(stream_key, 2), amount)]


def centred(own_key, dims, spread, most, cuts=(), held_as=jnp.bfloat16):
    entries = jax.random.normal(own_key, dims, jnp.float32) * spread
    if len(cuts) > 0:
        entries = block_levels(own_key, dims, cuts, -0.22, 0.18) * entries
    return jnp.clip(entries, min=-most, max=most).astype(held_as)


def setup_inputs(seed: int = 0) -> dict:
    streams_of = jax.random.split(jax.random.key(seed), 9)
    return {
        "resid": draw_resid(jax.random.fold_in(streams_of[8], 71), 0),
        "norm_gain": jnp.clip(1.0 + 0.1 * jax.random.normal(streams_of[1], (D,), jnp.float32), 0.5, 1.5).astype(jnp.bfloat16),
        "cotangent": centred(streams_of[2], (TOKENS, 2, R), 0.01, 0.059814453, ((0, 8),)),
        "segment_ids": jax.vmap(lambda own: jnp.searchsorted(jnp.cumsum(ragged(own, CAND_DEV, TOK_DEV, min(TOK_DEV - CAND_DEV + 1, 2 * TOK_DEV // CAND_DEV), 2)), jnp.arange(TOK_DEV), side="right"))(jax.random.split(streams_of[3], N_DP)).reshape((N_DP, TOK_DEV)).astype(jnp.int32),
        "query_grads": centred(streams_of[4], (NQ, 2, R, D), 0.002, 0.011962891, ((0, 8), (3, 64))),
        "input_basis": centred(streams_of[5], (2, D, D), D ** -0.5, 0.0625, ((1, 8), (2, 64))),
        "output_basis": centred(streams_of[6], (2, R, R), R ** -0.5, 0.75),
        "eigenvalues": draw_eigenvalues(jax.random.fold_in(streams_of[8], 71), 0),
    }


def reference(resid, norm_gain, cotangent, segment_ids, query_grads, input_basis, output_basis, eigenvalues):
    values = resid.astype(jnp.float32)
    mean_square = lax.optimization_barrier(jnp.mean(values * values, axis=1, keepdims=True))
    normed = (values * lax.rsqrt(mean_square + 1e-05) * norm_gain.astype(jnp.float32)).astype(jnp.bfloat16)
    owners = (segment_ids + (jnp.arange(N_DP, dtype=jnp.int32) * CAND_DEV)[:, None]).reshape(TOKENS)
    onehot = (owners[None, :] == jnp.arange(CANDS, dtype=jnp.int32)[:, None]).astype(jnp.float32)
    weighted = onehot[:, :, None, None] * cotangent.astype(jnp.float32)[None]
    grads = jnp.einsum('stmb,ti->smbi', weighted, normed.astype(jnp.float32)).astype(jnp.bfloat16)
    stacked = jnp.concatenate([grads, query_grads], axis=0)
    count = CANDS + NQ
    scores = jnp.zeros((CANDS, NQ), jnp.float32)
    for module in range(2):
        flat = stacked[:, module].reshape(count * R, D)
        inner = jnp.dot(flat, input_basis[module], preferred_element_type=jnp.float32).reshape(count, R, D)
        turned = jnp.einsum('ba,nbj->naj', output_basis[module].astype(jnp.float32), inner, precision=lax.Precision.HIGHEST)
        damping = 0.1 * jnp.mean(eigenvalues[module])
        weights = turned[:CANDS] / (eigenvalues[module] + damping)
        scores = scores + jnp.einsum('saj,qaj->sq', weights, turned[CANDS:], precision=lax.Precision.HIGHEST)
    return scores
```

```python
import jax
import jax.numpy as jnp
from jax import lax
from jax.sharding import Mesh, PartitionSpec as P

D = 8192
R = 64
MODULES = 2
CAND_DEV = 2
Q_DEV = 2
STACK = CAND_DEV + Q_DEV
FACTOR = ("x", "core")
GROUPS = 8
A_ROWS = MODULES * R // GROUPS


def split_three(value):
    high = value.astype(jnp.bfloat16)
    rest = value - high.astype(jnp.float32)
    middle = rest.astype(jnp.bfloat16)
    low = (rest - middle.astype(jnp.float32)).astype(jnp.bfloat16)
    return jnp.stack([high, middle, low])


def body(
    resid, norm_gain, cotangent, segment_ids, query_grads, input_basis, output_basis, eigenvalues
):
    n_dp = lax.axis_size("dp")
    n_t = lax.axis_size("tensor")
    t = lax.axis_index("tensor")
    group = lax.axis_index(FACTOR)
    tokens, width = resid.shape

    basis = lax.all_gather(input_basis, FACTOR, axis=0)

    values = resid.astype(jnp.float32)
    squares = jnp.sum(values * values, axis=1)
    per_t = A_ROWS // n_t
    eigen_part = lax.dynamic_index_in_dim(
        eigenvalues.reshape(GROUPS, n_t, per_t * width), t, axis=1, keepdims=False
    )
    parcel = jnp.concatenate(
        [
            jnp.broadcast_to(squares, (n_t, GROUPS, tokens)),
            jnp.broadcast_to(eigen_part, (n_t, GROUPS, per_t * width)),
        ],
        axis=2,
    ).reshape(n_t * GROUPS, 1, tokens + per_t * width)
    parcel = lax.all_to_all(parcel, ("tensor",) + FACTOR, 0, 0, tiled=True)
    totals = jnp.sum(parcel[:, 0, :tokens], axis=0)
    eigen = lax.dynamic_index_in_dim(
        parcel.reshape(n_t, GROUPS, tokens + per_t * width)[:, :, tokens:], t, axis=1, keepdims=False
    ).reshape(A_ROWS, width)

    normed = (
        values * lax.rsqrt(totals / D + 1e-05)[:, None] * norm_gain.astype(jnp.float32)
    ).astype(jnp.bfloat16)
    onehot = (
        segment_ids[0][None, :] == jnp.arange(CAND_DEV, dtype=jnp.int32)[:, None]
    ).astype(jnp.bfloat16)
    weighted = onehot[:, :, None, None] * cotangent[None]
    grads = jnp.einsum(
        "stmb,ti->smbi", weighted, normed, preferred_element_type=jnp.float32
    ).astype(jnp.bfloat16)
    stack = jnp.concatenate([grads, query_grads], axis=0)
    turned = jnp.einsum(
        "mba,nmbi->mani", output_basis, stack, preferred_element_type=jnp.float32
    ).astype(jnp.bfloat16)
    turned = turned.reshape(GROUPS, A_ROWS * STACK, width)
    eigen_sums = split_three(jnp.sum(eigenvalues, axis=(1, 2)))
    extra = jnp.zeros((8, width), jnp.bfloat16).at[:3, :MODULES].set(eigen_sums)
    rows = jnp.concatenate(
        [turned, jnp.broadcast_to(extra, (GROUPS, 8, width))], axis=1
    )
    rows = jnp.broadcast_to(rows, (n_dp,) + rows.shape).reshape((n_dp * GROUPS,) + rows.shape[1:])
    rows = lax.all_to_all(rows, ("dp",) + FACTOR, 0, 0, tiled=True)
    sums = jnp.sum(rows[:, A_ROWS * STACK : A_ROWS * STACK + 3, :MODULES].astype(jnp.float32), axis=(0, 1))
    damping = 0.1 * sums / (R * D)
    rows = rows[:, : A_ROWS * STACK].reshape(n_dp, GROUPS, A_ROWS * STACK, width)

    module = group // (GROUPS // MODULES)
    mine = lax.dynamic_index_in_dim(basis, module, axis=1, keepdims=False)
    mine = mine.reshape(GROUPS, GROUPS, width, mine.shape[-1])
    partial = jnp.einsum(
        "dfrk,hfkj->hdrj", rows, mine, preferred_element_type=jnp.float32
    ).astype(jnp.bfloat16)
    columns = partial.shape[-1]
    partial = partial.reshape(GROUPS, n_dp * A_ROWS * STACK, columns)
    partial = lax.all_to_all(partial, "tensor", 0, 0, tiled=True)
    rotated = jnp.sum(partial.astype(jnp.float32), axis=0)
    rotated = rotated.reshape(n_dp, A_ROWS, STACK, columns)

    weight = 1.0 / (eigen + lax.dynamic_index_in_dim(damping, module, keepdims=False))
    candidates = rotated[:, :, :CAND_DEV] * weight[None, :, None, :]
    queries = rotated[:, :, CAND_DEV:]
    scores = jnp.einsum(
        "dasj,eaqj->dseq", candidates, queries, precision=lax.Precision.HIGHEST
    ).reshape(2, -1)
    scores = lax.psum(scores, "core")
    peers = n_dp * n_t * lax.axis_size("x")
    scores = jnp.broadcast_to(scores, (peers,) + scores.shape)
    scores = lax.all_to_all(scores, ("dp", "tensor", "x"), 0, 0, tiled=True)
    return jnp.sum(scores, axis=0).reshape(n_dp * CAND_DEV, n_dp * Q_DEV)


def solution(mesh):
    n_dp, n_t, n_f = (mesh.shape[name] for name in ("dp", "tensor", "factor"))
    fine = Mesh(mesh.devices.reshape(n_dp, n_t, n_f // 2, 2), ("dp", "tensor", "x", "core"))
    placed = (
        P("dp", ("tensor", "x", "core")),
        P(("tensor", "x", "core")),
        P("dp", None, None),
        P("dp", None),
        P("dp", None, None, ("tensor", "x", "core")),
        P(None, "tensor", ("dp", "x", "core")),
        P(),
        P(None, None, ("dp", "x", "core")),
    )
    return jax.shard_map(body, mesh=fine, in_specs=placed, out_specs=P(), check_vma=False)
```

```python
import jax
import jax.numpy as jnp
from jax import lax
from jax.sharding import Mesh, PartitionSpec as P

D = 8192
R = 64
MODULES = 2
CAND_DEV = 2
DP = ("zh", "zl")
FACTOR = ("x", "core")


def split_three(value):
    high = value.astype(jnp.bfloat16)
    rest = value - high.astype(jnp.float32)
    middle = rest.astype(jnp.bfloat16)
    low = (rest - middle.astype(jnp.float32)).astype(jnp.bfloat16)
    return jnp.stack([high, middle, low])


def everywhere(value, axes):
    peers = 1
    for axis in axes:
        peers *= lax.axis_size(axis)
    terms = jnp.broadcast_to(value, (peers,) + value.shape)
    return jnp.sum(lax.all_to_all(terms, axes, 0, 0, tiled=True), axis=0)


def body(
    resid, norm_gain, cotangent, segment_ids, query_grads, input_basis, output_basis, eigenvalues
):
    n_zh, n_zl = lax.axis_size("zh"), lax.axis_size("zl")
    n_t, n_x, n_c = lax.axis_size("tensor"), lax.axis_size("x"), lax.axis_size("core")
    n_dp, n_f = n_zh * n_zl, n_x * n_c
    module = lax.axis_index("zl")
    t = lax.axis_index("tensor")
    core = lax.axis_index("core")
    tokens, width = resid.shape
    a_rows = R // n_x
    rows_dev = a_rows * CAND_DEV

    basis = lax.all_gather(input_basis, ("zl", "x"), axis=0)

    swap = []
    for zl in range(n_zl):
        for tt in range(n_t):
            for x in range(n_x):
                source = ((tt // n_x) * n_t + zl * n_x + x) * n_x + tt % n_x
                swap.append((source, (zl * n_t + tt) * n_x + x))
    eigen_part = lax.dynamic_index_in_dim(
        eigenvalues.reshape(n_t, a_rows, width), t, axis=0, keepdims=False
    )
    eigen = lax.ppermute(eigen_part, ("zl", "tensor", "x"), swap)

    values = resid.astype(jnp.float32)
    squares = jnp.sum(values * values, axis=1)
    totals = everywhere(squares.reshape(-1, 128), ("tensor",) + FACTOR).reshape(-1)

    normed = (
        values * lax.rsqrt(totals / D + 1e-05)[:, None] * norm_gain.astype(jnp.float32)
    ).astype(jnp.bfloat16)
    onehot = (
        segment_ids[0][None, :] == jnp.arange(CAND_DEV, dtype=jnp.int32)[:, None]
    ).astype(jnp.bfloat16)
    weighted = onehot[:, :, None, None] * cotangent[None]
    grads = jnp.einsum(
        "stmb,ti->smbi", weighted, normed, preferred_element_type=jnp.float32
    ).astype(jnp.bfloat16)
    stack = jnp.stack([grads, query_grads])
    turned = jnp.einsum(
        "mbxa,hnmbi->mxhnai",
        output_basis.reshape(MODULES, R, n_x, a_rows),
        stack,
        preferred_element_type=jnp.float32,
    ).astype(jnp.bfloat16)
    turned = turned.reshape(MODULES, n_x, n_c, rows_dev, width)
    eigen_sums = split_three(jnp.sum(eigenvalues, axis=(1, 2)))
    extra = jnp.zeros((8, width), jnp.bfloat16).at[:3, :MODULES].set(eigen_sums)
    parcel = jnp.concatenate(
        [turned, jnp.broadcast_to(extra, (MODULES, n_x, n_c) + extra.shape)], axis=3
    )
    parcel = jnp.broadcast_to(parcel, (n_zh,) + parcel.shape)
    parcel = parcel.reshape((n_dp * n_f,) + parcel.shape[-2:])
    parcel = lax.all_to_all(parcel, DP + FACTOR, 0, 0, tiled=True)
    sums = jnp.sum(parcel[:, rows_dev : rows_dev + 3, :MODULES].astype(jnp.float32), axis=(0, 1))
    damping = 0.1 * sums / (R * D)

    mine = parcel[:, :rows_dev]
    other = lax.ppermute(mine, "core", [(0, 1), (1, 0)])
    blocks = lax.dynamic_index_in_dim(basis, module, axis=1, keepdims=False)
    blocks = blocks.reshape(n_t, n_f, width, blocks.shape[-1])

    def rotate(rows):
        return jnp.einsum(
            "dfrk,hfkj->hdrj",
            rows.reshape(n_dp, n_f, rows_dev, width),
            blocks,
            preferred_element_type=jnp.float32,
        ).astype(jnp.bfloat16)

    partial = jnp.stack([rotate(mine), rotate(other)], axis=1)
    partial = partial.reshape(n_t, 2 * n_dp * rows_dev, -1)
    partial = lax.all_to_all(partial, "tensor", 0, 0, tiled=True)
    rotated = jnp.sum(partial.astype(jnp.float32), axis=0)
    rotated = rotated.reshape(2, n_dp * CAND_DEV, a_rows, -1)

    weight = 1.0 / (eigen + lax.dynamic_index_in_dim(damping, module, keepdims=False))
    scores = jnp.einsum(
        "naj,kaj->nk", rotated[0] * weight, rotated[1], precision=lax.Precision.HIGHEST
    )
    shape = scores.shape
    scores = jnp.where(core == 0, scores, scores.T).reshape(2, -1)
    scores = lax.psum(scores, "core")
    scores = everywhere(scores, ("tensor", "x"))
    return everywhere(scores, DP).reshape(shape)


def solution(mesh):
    n_dp, n_t, n_f = (mesh.shape[name] for name in ("dp", "tensor", "factor"))
    fine = Mesh(
        mesh.devices.reshape(n_dp // 2, 2, n_t, n_f // 2, 2), DP + ("tensor",) + FACTOR
    )
    features = ("tensor",) + FACTOR
    columns = DP + FACTOR
    placed = (
        P(DP, features),
        P(features),
        P(DP, None, None),
        P(DP, None),
        P(DP, None, None, features),
        P(None, "tensor", columns),
        P(),
        P(None, None, columns),
    )
    return jax.shard_map(body, mesh=fine, in_specs=placed, out_specs=P(), check_vma=False)
```

```python
import jax
import jax.numpy as jnp
from jax import lax
from jax.experimental import pallas as pl
from jax.experimental.pallas import tpu as pltpu
from jax.sharding import Mesh, PartitionSpec as P

D = 8192
R = 64
MODULES = 2
CAND_DEV = 2
DP = ("zh", "zl")
FACTOR = ("x", "core")


def split_three(value):
    high = value.astype(jnp.bfloat16)
    rest = value - high.astype(jnp.float32)
    middle = rest.astype(jnp.bfloat16)
    low = (rest - middle.astype(jnp.float32)).astype(jnp.bfloat16)
    return jnp.stack([high, middle, low])


def everywhere(value, axes):
    peers = 1
    for axis in axes:
        peers *= lax.axis_size(axis)
    terms = jnp.broadcast_to(value, (peers,) + value.shape)
    return jnp.sum(lax.all_to_all(terms, axes, 0, 0, tiled=True), axis=0)


def rotate_kernel(mine_ref, other_ref, *refs):
    *block_refs, out_ref, rows_ref = refs
    sources, height, width = mine_ref.shape
    across = rows_ref.shape[1] // width
    for half, ref in enumerate((mine_ref, other_ref)):
        for source in range(sources):
            top = (half * (sources // across) + source // across) * height
            left = (source % across) * width
            rows_ref[top : top + height, left : left + width] = ref[source]
    shifts = len(block_refs)
    for shift, ref in enumerate(block_refs):
        columns = jnp.concatenate([ref[0], ref[1]], axis=1)
        product = jnp.dot(rows_ref[...], columns, preferred_element_type=jnp.float32)
        out_ref[shift] = product[:, :width].astype(jnp.bfloat16)
        out_ref[shifts + shift] = product[:, width:].astype(jnp.bfloat16)


def body(
    resid, norm_gain, cotangent, segment_ids, query_grads, input_basis, output_basis, eigenvalues
):
    n_zh, n_zl = lax.axis_size("zh"), lax.axis_size("zl")
    n_t, n_x, n_c = lax.axis_size("tensor"), lax.axis_size("x"), lax.axis_size("core")
    n_dp, n_f = n_zh * n_zl, n_x * n_c
    module = lax.axis_index("zl")
    t = lax.axis_index("tensor")
    core = lax.axis_index("core")
    tokens, width = resid.shape
    a_rows = R // n_x
    rows_dev = a_rows * CAND_DEV

    own = lax.dynamic_index_in_dim(input_basis, module, axis=0, keepdims=False)
    got = lax.ppermute(
        lax.dynamic_index_in_dim(input_basis, 1 - module, axis=0, keepdims=False),
        "zl",
        [(0, 1), (1, 0)],
    )
    pair = jnp.stack([own, got])
    moves = []
    for zl in range(n_zl):
        for h in range(n_t):
            for x in range(n_x):
                source = ((zl ^ (h // n_x)) * n_t + h) * n_x + (x + h % n_x) % n_x
                moves.append((source, (zl * n_t + h) * n_x + x))
    wanted = jnp.bitwise_xor(module, t // n_x) * n_x + (lax.axis_index("x") - t % n_x) % n_x
    eigen_part = lax.dynamic_index_in_dim(
        eigenvalues.reshape(MODULES * n_x, a_rows, width), wanted, axis=0, keepdims=False
    )
    eigen = lax.ppermute(eigen_part, ("zl", "tensor", "x"), moves)

    values = resid.astype(jnp.float32)
    squares = jnp.sum(values * values, axis=1)
    totals = everywhere(squares.reshape(-1, 128), ("tensor",) + FACTOR).reshape(-1)

    totals, pair = lax.optimization_barrier((totals, pair))
    blocks = [pair] + [
        lax.ppermute(pair, "x", [((x + step) % n_x, x) for x in range(n_x)])
        for step in range(1, n_x)
    ]

    normed = (
        values * lax.rsqrt(totals / D + 1e-05)[:, None] * norm_gain.astype(jnp.float32)
    ).astype(jnp.bfloat16)
    onehot = (
        segment_ids[0][None, :] == jnp.arange(CAND_DEV, dtype=jnp.int32)[:, None]
    ).astype(jnp.bfloat16)
    weighted = onehot[:, :, None, None] * cotangent[None]
    grads = jnp.einsum(
        "stmb,ti->smbi", weighted, normed, preferred_element_type=jnp.float32
    ).astype(jnp.bfloat16)
    stack = jnp.stack([grads, query_grads])
    turned = jnp.einsum(
        "mbxa,hnmbi->mxhnai",
        output_basis.reshape(MODULES, R, n_x, a_rows),
        stack,
        preferred_element_type=jnp.float32,
    ).astype(jnp.bfloat16)
    turned = turned.reshape(MODULES, n_x, n_c, rows_dev, width)
    eigen_sums = split_three(jnp.sum(eigenvalues, axis=(1, 2)))
    extra = jnp.zeros((8, width), jnp.bfloat16).at[:3, :MODULES].set(eigen_sums)
    parcel = jnp.concatenate(
        [turned, jnp.broadcast_to(extra, (MODULES, n_x, n_c) + extra.shape)], axis=3
    )
    parcel = jnp.broadcast_to(parcel, (n_zh,) + parcel.shape)
    parcel = parcel.reshape((n_dp * n_f,) + parcel.shape[-2:])
    parcel = lax.all_to_all(parcel, DP + FACTOR, 0, 0, tiled=True)
    sums = jnp.sum(parcel[:, rows_dev : rows_dev + 3, :MODULES].astype(jnp.float32), axis=(0, 1))
    damping = 0.1 * sums / (R * D)

    mine = parcel[:, :rows_dev]
    other = lax.ppermute(mine, "core", [(0, 1), (1, 0)])
    partial = pl.pallas_call(
        rotate_kernel,
        out_shape=jax.ShapeDtypeStruct((n_t, 2 * n_dp * rows_dev, 128), jnp.bfloat16),
        in_specs=[pl.BlockSpec(memory_space=pltpu.VMEM)] * (2 + n_x),
        out_specs=pl.BlockSpec(memory_space=pltpu.VMEM),
        scratch_shapes=[pltpu.VMEM((2 * n_dp * rows_dev, n_f * width), jnp.bfloat16)],
        compiler_params=pltpu.CompilerParams(vmem_limit_bytes=32 << 20),
        name="rotate",
    )(mine, other, *blocks)
    partial = lax.all_to_all(partial, "tensor", 0, 0, tiled=True)
    rotated = jnp.sum(partial.astype(jnp.float32), axis=0)
    rotated = rotated.reshape(2, n_dp * CAND_DEV, a_rows, -1)

    weight = 1.0 / (eigen + lax.dynamic_index_in_dim(damping, module, keepdims=False))
    scores = jnp.einsum(
        "naj,kaj->nk", rotated[0] * weight, rotated[1], precision=lax.Precision.HIGHEST
    )
    shape = scores.shape
    scores = jnp.where(core == 0, scores, scores.T).reshape(2, -1)
    scores = lax.psum(scores, "core")
    return everywhere(scores, DP + ("tensor", "x")).reshape(shape)


def solution(mesh):
    n_dp, n_t, n_f = (mesh.shape[name] for name in ("dp", "tensor", "factor"))
    fine = Mesh(
        mesh.devices.reshape(n_dp // 2, 2, n_t, n_f // 2, 2), DP + ("tensor",) + FACTOR
    )
    features = ("tensor",) + FACTOR
    columns = DP + FACTOR
    placed = (
        P(DP, features),
        P(features),
        P(DP, None, None),
        P(DP, None),
        P(DP, None, None, features),
        P(None, "tensor", columns),
        P(),
        P(None, None, columns),
    )
    return jax.shard_map(body, mesh=fine, in_specs=placed, out_specs=P(), check_vma=False)
```

```python
import jax
import jax.numpy as jnp
from jax import lax
from jax.experimental import pallas as pl
from jax.experimental.pallas import tpu as pltpu
from jax.sharding import Mesh, PartitionSpec as P

D = 8192
R = 64
MODULES = 2
CAND_DEV = 2
DP = ("zh", "zl")
FACTOR = ("x", "core")


def split_three(value):
    high = value.astype(jnp.bfloat16)
    rest = value - high.astype(jnp.float32)
    middle = rest.astype(jnp.bfloat16)
    low = (rest - middle.astype(jnp.float32)).astype(jnp.bfloat16)
    return jnp.stack([high, middle, low])


def everywhere(value, axes):
    peers = 1
    for axis in axes:
        peers *= lax.axis_size(axis)
    terms = jnp.broadcast_to(value, (peers,) + value.shape)
    return jnp.sum(lax.all_to_all(terms, axes, 0, 0, tiled=True), axis=0)


def rotate_kernel(mine_ref, other_ref, *refs):
    *block_refs, out_ref, rows_ref = refs
    sources, height, width = mine_ref.shape
    across = rows_ref.shape[1] // width
    count = sources // across * height
    for half, ref in enumerate((mine_ref, other_ref)):
        for source in range(sources):
            top = half * count + source // across * height
            left = (source % across) * width
            rows_ref[top : top + height, left : left + width] = ref[source]
    shifts = len(block_refs)
    for shift, ref in enumerate(block_refs):
        columns = jnp.concatenate([ref[0], ref[1]], axis=1)
        product = jnp.dot(rows_ref[...], columns, preferred_element_type=jnp.float32)
        for near in range(2):
            part = product[:, near * width : (near + 1) * width].astype(jnp.bfloat16)
            out_ref[near * shifts + shift, :, :width] = part[:count]
            out_ref[near * shifts + shift, :, width:] = part[count:]


def body(
    resid, norm_gain, cotangent, segment_ids, query_grads, input_basis, output_basis, eigenvalues
):
    n_zh, n_zl = lax.axis_size("zh"), lax.axis_size("zl")
    n_t, n_x, n_c = lax.axis_size("tensor"), lax.axis_size("x"), lax.axis_size("core")
    n_dp, n_f = n_zh * n_zl, n_x * n_c
    module = lax.axis_index("zl")
    t = lax.axis_index("tensor")
    core = lax.axis_index("core")
    tokens, width = resid.shape
    a_rows = R // n_x
    rows_dev = a_rows * CAND_DEV

    own = lax.dynamic_index_in_dim(input_basis, module, axis=0, keepdims=False)
    got = lax.ppermute(
        lax.dynamic_index_in_dim(input_basis, 1 - module, axis=0, keepdims=False),
        "zl",
        [(0, 1), (1, 0)],
    )
    values = resid.astype(jnp.float32)
    squares = jnp.sum(values * values, axis=1)
    squares, got = lax.optimization_barrier((squares, got))
    pair = jnp.stack([own, got])
    blocks = [pair] + [
        lax.ppermute(pair, "x", [((x + step) % n_x, x) for x in range(n_x)])
        for step in range(1, n_x)
    ]
    moves = []
    for zl in range(n_zl):
        for h in range(n_t):
            for x in range(n_x):
                source = ((zl ^ (h // n_x)) * n_t + h) * n_x + (x + h % n_x) % n_x
                moves.append((source, (zl * n_t + h) * n_x + x))
    wanted = jnp.bitwise_xor(module, t // n_x) * n_x + (lax.axis_index("x") - t % n_x) % n_x
    eigen_part = lax.dynamic_index_in_dim(
        eigenvalues.reshape(MODULES * n_x, a_rows, width), wanted, axis=0, keepdims=False
    )
    eigen = lax.ppermute(eigen_part, ("zl", "tensor", "x"), moves)

    totals = everywhere(squares.reshape(-1, 128), ("tensor",) + FACTOR).reshape(-1)

    normed = (
        values * lax.rsqrt(totals / D + 1e-05)[:, None] * norm_gain.astype(jnp.float32)
    ).astype(jnp.bfloat16)
    onehot = (
        segment_ids[0][None, :] == jnp.arange(CAND_DEV, dtype=jnp.int32)[:, None]
    ).astype(jnp.bfloat16)
    weighted = onehot[:, :, None, None] * cotangent[None]
    grads = jnp.einsum(
        "stmb,ti->smbi", weighted, normed, preferred_element_type=jnp.float32
    ).astype(jnp.bfloat16)
    stack = jnp.stack([grads, query_grads])
    turned = jnp.einsum(
        "mbxa,hnmbi->mxhnai",
        output_basis.reshape(MODULES, R, n_x, a_rows),
        stack,
        preferred_element_type=jnp.float32,
    ).astype(jnp.bfloat16)
    turned = turned.reshape(MODULES, n_x, n_c, rows_dev, width)
    eigen_sums = split_three(jnp.sum(eigenvalues, axis=(1, 2)))
    extra = jnp.zeros((8, width), jnp.bfloat16).at[:3, :MODULES].set(eigen_sums)
    parcel = jnp.concatenate(
        [turned, jnp.broadcast_to(extra, (MODULES, n_x, n_c) + extra.shape)], axis=3
    )
    parcel = jnp.broadcast_to(parcel, (n_zh,) + parcel.shape)
    parcel = parcel.reshape((n_dp * n_f,) + parcel.shape[-2:])
    parcel, blocks[1] = lax.optimization_barrier((parcel, blocks[1]))
    parcel = lax.all_to_all(parcel, DP + FACTOR, 0, 0, tiled=True)
    sums = jnp.sum(parcel[:, rows_dev : rows_dev + 3, :MODULES].astype(jnp.float32), axis=(0, 1))
    damping = 0.1 * sums / (R * D)

    mine = parcel[:, :rows_dev]
    other = lax.ppermute(mine, "core", [(0, 1), (1, 0)])
    partial = pl.pallas_call(
        rotate_kernel,
        out_shape=jax.ShapeDtypeStruct((n_t, n_dp * rows_dev, 2 * width), jnp.bfloat16),
        in_specs=[pl.BlockSpec(memory_space=pltpu.VMEM)] * (2 + n_x),
        out_specs=pl.BlockSpec(memory_space=pltpu.VMEM),
        scratch_shapes=[pltpu.VMEM((2 * n_dp * rows_dev, n_f * width), jnp.bfloat16)],
        compiler_params=pltpu.CompilerParams(vmem_limit_bytes=32 << 20),
        name="rotate",
    )(mine, other, *blocks)
    partial = lax.all_to_all(partial, "tensor", 0, 0, tiled=True)
    rotated = jnp.sum(partial.astype(jnp.float32), axis=0)
    halves = (n_dp * CAND_DEV, a_rows, width)
    first = rotated[:, :width].reshape(halves)
    second = rotated[:, width:].reshape(halves)

    weight = 1.0 / (eigen + lax.dynamic_index_in_dim(damping, module, keepdims=False))
    scores = jnp.einsum(
        "naj,kaj->nk", first * weight, second, precision=lax.Precision.HIGHEST
    )
    shape = scores.shape
    scores = jnp.where(core == 0, scores, scores.T).reshape(2, -1)
    scores = lax.psum(scores, "core")
    return everywhere(scores, DP + ("tensor", "x")).reshape(shape)


def solution(mesh):
    n_dp, n_t, n_f = (mesh.shape[name] for name in ("dp", "tensor", "factor"))
    fine = Mesh(
        mesh.devices.reshape(n_dp // 2, 2, n_t, n_f // 2, 2), DP + ("tensor",) + FACTOR
    )
    features = ("tensor",) + FACTOR
    columns = DP + FACTOR
    placed = (
        P(DP, features),
        P(features),
        P(DP, None, None),
        P(DP, None),
        P(DP, None, None, features),
        P(None, "tensor", columns),
        P(),
        P(None, None, columns),
    )
    return jax.shard_map(body, mesh=fine, in_specs=placed, out_specs=P(), check_vma=False)
```

```python
import jax
import jax.numpy as jnp
from jax import lax
from jax.experimental import pallas as pl
from jax.experimental.pallas import tpu as pltpu
from jax.sharding import Mesh, PartitionSpec as P

D = 8192
R = 64
MODULES = 2
CAND_DEV = 2
DP = ("zh", "zl")
FACTOR = ("x", "core")


def split_three(value):
    high = value.astype(jnp.bfloat16)
    rest = value - high.astype(jnp.float32)
    middle = rest.astype(jnp.bfloat16)
    low = (rest - middle.astype(jnp.float32)).astype(jnp.bfloat16)
    return jnp.stack([high, middle, low])


def everywhere(value, axes):
    peers = 1
    for axis in axes:
        peers *= lax.axis_size(axis)
    terms = jnp.broadcast_to(value, (peers,) + value.shape)
    return jnp.sum(lax.all_to_all(terms, axes, 0, 0, tiled=True), axis=0)


def rotate_kernel(mine_ref, other_ref, blocks_ref, out_ref, rows_ref):
    sources, height, width = mine_ref.shape
    across = rows_ref.shape[1] // width
    for half, ref in enumerate((mine_ref, other_ref)):
        for source in range(sources):
            top = (half * (sources // across) + source // across) * height
            left = (source % across) * width
            rows_ref[top : top + height, left : left + width] = ref[source]
    shifts = blocks_ref.shape[0]
    for shift in range(shifts):
        columns = jnp.concatenate([blocks_ref[shift, 0], blocks_ref[shift, 1]], axis=1)
        product = jnp.dot(rows_ref[...], columns, preferred_element_type=jnp.float32)
        out_ref[shift] = product[:, :width].astype(jnp.bfloat16)
        out_ref[shifts + shift] = product[:, width:].astype(jnp.bfloat16)


def body(
    resid, norm_gain, cotangent, segment_ids, query_grads, input_basis, output_basis, eigenvalues
):
    n_zh, n_zl = lax.axis_size("zh"), lax.axis_size("zl")
    n_t, n_x, n_c = lax.axis_size("tensor"), lax.axis_size("x"), lax.axis_size("core")
    n_dp, n_f = n_zh * n_zl, n_x * n_c
    module = lax.axis_index("zl")
    t = lax.axis_index("tensor")
    core = lax.axis_index("core")
    tokens, width = resid.shape
    a_rows = R // n_x
    rows_dev = a_rows * CAND_DEV

    own = lax.dynamic_index_in_dim(input_basis, module, axis=0, keepdims=False)
    got = lax.ppermute(
        lax.dynamic_index_in_dim(input_basis, 1 - module, axis=0, keepdims=False),
        "zl",
        [(0, 1), (1, 0)],
    )
    pair = jnp.stack([own, got])
    moves = []
    for zl in range(n_zl):
        for h in range(n_t):
            for x in range(n_x):
                source = ((zl ^ (h // n_x)) * n_t + h // n_x * n_x + x) * n_x + h % n_x
                moves.append((source, (zl * n_t + h) * n_x + x))
    wanted = jnp.bitwise_xor(module, t // n_x) * n_x + t % n_x
    eigen_part = lax.dynamic_index_in_dim(
        eigenvalues.reshape(MODULES * n_x, a_rows, width), wanted, axis=0, keepdims=False
    )
    eigen = lax.ppermute(eigen_part, ("zl", "tensor", "x"), moves)

    values = resid.astype(jnp.float32)
    squares = jnp.sum(values * values, axis=1)
    totals = everywhere(squares.reshape(-1, 128), ("tensor",) + FACTOR).reshape(-1)

    eigen_sums = split_three(jnp.sum(eigenvalues, axis=(1, 2)))
    extra = jnp.zeros((8, width), jnp.bfloat16).at[:3, :MODULES].set(eigen_sums)
    totals, pair, extra = lax.optimization_barrier((totals, pair, extra))
    blocks = lax.all_gather(pair, "x", axis=0)

    normed = (
        values * lax.rsqrt(totals / D + 1e-05)[:, None] * norm_gain.astype(jnp.float32)
    ).astype(jnp.bfloat16)
    onehot = (
        segment_ids[0][None, :] == jnp.arange(CAND_DEV, dtype=jnp.int32)[:, None]
    ).astype(jnp.bfloat16)
    weighted = onehot[:, :, None, None] * cotangent[None]
    grads = jnp.einsum(
        "stmb,ti->smbi", weighted, normed, preferred_element_type=jnp.float32
    ).astype(jnp.bfloat16)
    stack = jnp.stack([grads, query_grads])
    turned = jnp.einsum(
        "mbxa,hnmbi->mxhnai",
        output_basis.reshape(MODULES, R, n_x, a_rows),
        stack,
        preferred_element_type=jnp.float32,
    ).astype(jnp.bfloat16)
    turned = turned.reshape(MODULES, n_x, n_c, rows_dev, width)
    parcel = jnp.concatenate(
        [turned, jnp.broadcast_to(extra, (MODULES, n_x, n_c) + extra.shape)], axis=3
    )
    parcel = jnp.broadcast_to(parcel, (n_zh,) + parcel.shape)
    parcel = parcel.reshape((n_dp * n_f,) + parcel.shape[-2:])
    parcel = lax.all_to_all(parcel, DP + FACTOR, 0, 0, tiled=True)
    sums = jnp.sum(parcel[:, rows_dev : rows_dev + 3, :MODULES].astype(jnp.float32), axis=(0, 1))
    damping = 0.1 * sums / (R * D)

    mine = parcel[:, :rows_dev]
    other = lax.ppermute(mine, "core", [(0, 1), (1, 0)])
    partial = pl.pallas_call(
        rotate_kernel,
        out_shape=jax.ShapeDtypeStruct((n_t, 2 * n_dp * rows_dev, 128), jnp.bfloat16),
        in_specs=[pl.BlockSpec(memory_space=pltpu.VMEM)] * 3,
        out_specs=pl.BlockSpec(memory_space=pltpu.VMEM),
        scratch_shapes=[pltpu.VMEM((2 * n_dp * rows_dev, n_f * width), jnp.bfloat16)],
        compiler_params=pltpu.CompilerParams(vmem_limit_bytes=32 << 20),
        name="rotate",
    )(mine, other, blocks)
    partial = lax.all_to_all(partial, "tensor", 0, 0, tiled=True)
    rotated = jnp.sum(partial.astype(jnp.float32), axis=0)
    rotated = rotated.reshape(2, n_dp * CAND_DEV, a_rows, -1)

    weight = 1.0 / (eigen + lax.dynamic_index_in_dim(damping, module, keepdims=False))
    scores = jnp.einsum(
        "naj,kaj->nk", rotated[0] * weight, rotated[1], precision=lax.Precision.HIGHEST
    )
    shape = scores.shape
    scores = jnp.where(core == 0, scores, scores.T).reshape(2, -1)
    scores = lax.psum(scores, "core")
    return everywhere(scores, DP + ("tensor", "x")).reshape(shape)


def solution(mesh):
    n_dp, n_t, n_f = (mesh.shape[name] for name in ("dp", "tensor", "factor"))
    fine = Mesh(
        mesh.devices.reshape(n_dp // 2, 2, n_t, n_f // 2, 2), DP + ("tensor",) + FACTOR
    )
    features = ("tensor",) + FACTOR
    columns = DP + FACTOR
    placed = (
        P(DP, features),
        P(features),
        P(DP, None, None),
        P(DP, None),
        P(DP, None, None, features),
        P(None, "tensor", columns),
        P(),
        P(None, None, columns),
    )
    return jax.shard_map(body, mesh=fine, in_specs=placed, out_specs=P(), check_vma=False)
```

```python
import math

import jax
import jax.numpy as jnp
from jax import lax
from jax.experimental import pallas as pl
from jax.experimental.pallas import tpu as pltpu
from jax.sharding import Mesh, PartitionSpec as P

D = 8192
R = 64
MODULES = 2
CAND_DEV = 2
FACTOR = ("x", "core")


def everywhere(value, axes):
    peers = math.prod(lax.axis_size(axis) for axis in axes)
    terms = jnp.broadcast_to(value, (peers,) + value.shape)
    return jnp.sum(lax.all_to_all(terms, axes, 0, 0, tiled=True), axis=0)


def prologue_kernel(resid_ref, eigen_ref, squares_ref, sums_ref):
    tokens, width = resid_ref.shape
    rows = []
    for top in range(0, tokens, width):
        values = resid_ref[top : top + width].astype(jnp.float32)
        rows.append(jnp.sum((values * values).T, axis=0, keepdims=True))
    squares_ref[...] = jnp.broadcast_to(jnp.concatenate(rows, axis=0), squares_ref.shape)
    terms = []
    for module in range(MODULES):
        rest = jnp.sum(eigen_ref[module], axis=0, keepdims=True)
        for _ in range(3):
            term = rest.astype(jnp.bfloat16).astype(jnp.float32)
            terms.append(term)
            rest = rest - term
    terms.append(jnp.zeros((sums_ref.shape[0] - 3 * MODULES, width), jnp.float32))
    sums_ref[...] = jnp.concatenate(terms, axis=0).astype(jnp.bfloat16)


def rotate_kernel(parcel_ref, near_ref, far_ref, out_ref, rows_ref):
    sources, _, width = parcel_ref.shape
    rows, depth = rows_ref.shape
    across = depth // width
    height = rows // 2 // (sources // across)
    for source in range(sources):
        for half in range(2):
            top = half * (rows // 2) + source // across * height
            left = (source % across) * width
            rows_ref[top : top + height, left : left + width] = parcel_ref[
                source, half * height : (half + 1) * height
            ]
    for shift in range(near_ref.shape[0]):
        columns = jnp.concatenate([near_ref[shift], far_ref[shift]], axis=1)
        product = jnp.dot(rows_ref[...], columns, preferred_element_type=jnp.float32)
        out_ref[2 * shift] = product[:, :width].astype(jnp.bfloat16)
        out_ref[2 * shift + 1] = product[:, width:].astype(jnp.bfloat16)


def body(
    resid, norm_gain, cotangent, segment_ids, query_grads, input_basis, output_basis, eigenvalues
):
    n_dp, n_t = lax.axis_size("dp"), lax.axis_size("tensor")
    n_x, n_c = lax.axis_size("x"), lax.axis_size("core")
    n_f = n_x * n_c
    t, x, core = lax.axis_index("tensor"), lax.axis_index("x"), lax.axis_index("core")
    tokens, width = resid.shape
    a_rows = MODULES * R // n_f
    rows_dev = 2 * CAND_DEV * a_rows

    module = x % MODULES

    own = lax.dynamic_index_in_dim(input_basis, module, axis=0, keepdims=False)
    rest = lax.dynamic_index_in_dim(input_basis, 1 - module, axis=0, keepdims=False)
    near = jnp.stack(
        [own]
        + [
            lax.ppermute(
                rest if step % MODULES else own, "x", [((k + step) % n_x, k) for k in range(n_x)]
            )
            for step in range(1, n_x)
        ]
    )
    far = lax.ppermute(near, "core", [(0, 1), (1, 0)])

    moves = []
    for h in range(n_t):
        for k in range(n_x):
            for c in range(n_c):
                source = (h * n_x + (k + h // n_c) % n_x) * n_c + (c ^ (h % n_c))
                moves.append((source, (h * n_x + k) * n_c + c))
    to_x = (x - t // n_c) % n_x
    wanted = (to_x % MODULES * (n_x // MODULES) + to_x // MODULES) * n_c + (core ^ (t % n_c))
    eigen_part = lax.dynamic_index_in_dim(
        eigenvalues.reshape(n_f, a_rows, width), wanted, axis=0, keepdims=False
    )
    eigen = lax.ppermute(eigen_part, ("tensor", "x", "core"), moves)

    squares, eigen_sums = pl.pallas_call(
        prologue_kernel,
        out_shape=(
            jax.ShapeDtypeStruct((n_t * n_f, tokens // width, width), jnp.float32),
            jax.ShapeDtypeStruct((8, width), jnp.bfloat16),
        ),
        in_specs=[pl.BlockSpec(memory_space=pltpu.VMEM)] * 2,
        out_specs=[pl.BlockSpec(memory_space=pltpu.VMEM)] * 2,
        name="prologue",
    )(resid, eigenvalues)
    squares = lax.all_to_all(squares, ("tensor",) + FACTOR, 0, 0, tiled=True)
    totals = jnp.sum(squares, axis=0).reshape(-1)

    values = resid.astype(jnp.float32)
    normed = (
        values * lax.rsqrt(totals / D + 1e-05)[:, None] * norm_gain.astype(jnp.float32)
    ).astype(jnp.bfloat16)
    onehot = (
        segment_ids[0][None, :] == jnp.arange(CAND_DEV, dtype=jnp.int32)[:, None]
    ).astype(jnp.bfloat16)
    weighted = onehot[:, :, None, None] * cotangent[None]
    grads = jnp.einsum(
        "stmb,ti->smbi", weighted, normed, preferred_element_type=jnp.float32
    ).astype(jnp.bfloat16)
    stack = jnp.concatenate([grads, query_grads], axis=0)
    turned = jnp.einsum(
        "mbxca,nmbi->xmcnai",
        output_basis.reshape(MODULES, R, n_x // MODULES, n_c, a_rows),
        stack,
        preferred_element_type=jnp.float32,
    ).astype(jnp.bfloat16)
    turned = turned.reshape(n_f, rows_dev, width)
    parcel = jnp.concatenate(
        [turned, jnp.broadcast_to(eigen_sums, (n_f,) + eigen_sums.shape)], axis=1
    )
    parcel = jnp.broadcast_to(parcel, (n_dp,) + parcel.shape)
    parcel = parcel.reshape((n_dp * n_f,) + parcel.shape[-2:])
    parcel = lax.all_to_all(parcel, ("dp",) + FACTOR, 0, 0, tiled=True)
    sums = parcel[:, rows_dev : rows_dev + 3 * MODULES].astype(jnp.float32)
    sums = jnp.sum(sums.reshape(-1, MODULES, 3 * width), axis=(0, 2))
    damping = 0.1 * sums / (R * D)

    partial = pl.pallas_call(
        rotate_kernel,
        out_shape=jax.ShapeDtypeStruct((n_t, n_dp * rows_dev, width), jnp.bfloat16),
        in_specs=[pl.BlockSpec(memory_space=pltpu.VMEM)] * 3,
        out_specs=pl.BlockSpec(memory_space=pltpu.VMEM),
        scratch_shapes=[pltpu.VMEM((n_dp * rows_dev, n_f * width), jnp.bfloat16)],
        compiler_params=pltpu.CompilerParams(vmem_limit_bytes=32 << 20),
        name="rotate",
    )(parcel, near, far)
    partial = lax.all_to_all(partial, "tensor", 0, 0, tiled=True)
    rotated = jnp.sum(partial.astype(jnp.float32), axis=0)
    rotated = rotated.reshape(2, n_dp * CAND_DEV, a_rows, width)

    weight = 1.0 / (eigen + lax.dynamic_index_in_dim(damping, module, keepdims=False))
    scores = jnp.einsum(
        "naj,kaj->nk", rotated[0] * weight, rotated[1], precision=lax.Precision.HIGHEST
    )
    shape = scores.shape
    scores = lax.psum(scores.reshape(2, -1), "core")
    return everywhere(scores, ("dp", "tensor", "x")).reshape(shape)


def solution(mesh):
    n_dp, n_t, n_f = (mesh.shape[name] for name in ("dp", "tensor", "factor"))
    fine = Mesh(mesh.devices.reshape(n_dp, n_t, n_f // 2, 2), ("dp", "tensor") + FACTOR)
    features = ("tensor",) + FACTOR
    columns = ("dp",) + FACTOR
    placed = (
        P("dp", features),
        P(features),
        P("dp", None, None),
        P("dp", None),
        P("dp", None, None, features),
        P(None, "tensor", columns),
        P(),
        P(None, None, columns),
    )
    return jax.shard_map(body, mesh=fine, in_specs=placed, out_specs=P(), check_vma=False)
```

```python
import functools
import math

import jax
import jax.numpy as jnp
from jax import lax
from jax.experimental import pallas as pl
from jax.experimental.pallas import tpu as pltpu
from jax.sharding import Mesh, PartitionSpec as P

D = 8192
R = 64
MODULES = 2
CAND_DEV = 2
FACTOR = ("x", "core")


def everywhere(value, axes):
    peers = math.prod(lax.axis_size(axis) for axis in axes)
    terms = jnp.broadcast_to(value, (peers,) + value.shape)
    return jnp.sum(lax.all_to_all(terms, axes, 0, 0, tiled=True), axis=0)


def prologue_kernel(resid_ref, eigen_ref, squares_ref, sums_ref):
    tokens, width = resid_ref.shape
    rows = []
    for top in range(0, tokens, width):
        values = resid_ref[top : top + width].astype(jnp.float32)
        rows.append(jnp.sum((values * values).T, axis=0, keepdims=True))
    squares_ref[...] = jnp.broadcast_to(jnp.concatenate(rows, axis=0), squares_ref.shape)
    terms = []
    for module in range(MODULES):
        rest = jnp.sum(eigen_ref[module], axis=0, keepdims=True)
        for _ in range(3):
            term = rest.astype(jnp.bfloat16).astype(jnp.float32)
            terms.append(term)
            rest = rest - term
    terms.append(jnp.zeros((sums_ref.shape[0] - 3 * MODULES, width), jnp.float32))
    sums_ref[...] = jnp.concatenate(terms, axis=0).astype(jnp.bfloat16)


def rotate_kernel(parcel_ref, near_ref, far_ref, out_ref, rows_ref):
    sources, _, width = parcel_ref.shape
    rows, depth = rows_ref.shape
    across = depth // width
    height = rows // 2 // (sources // across)
    for source in range(sources):
        for half in range(2):
            top = half * (rows // 2) + source // across * height
            left = (source % across) * width
            rows_ref[top : top + height, left : left + width] = parcel_ref[
                source, half * height : (half + 1) * height
            ]
    for shift in range(near_ref.shape[0]):
        columns = jnp.concatenate([near_ref[shift], far_ref[shift]], axis=1)
        product = jnp.dot(rows_ref[...], columns, preferred_element_type=jnp.float32)
        out_ref[2 * shift] = product[:, :width].astype(jnp.bfloat16)
        out_ref[2 * shift + 1] = product[:, width:].astype(jnp.bfloat16)


def body(
    resid, norm_gain, cotangent, segment_ids, query_grads, input_basis, output_basis, eigenvalues
):
    n_dp, n_t = lax.axis_size("dp"), lax.axis_size("tensor")
    n_x, n_c = lax.axis_size("x"), lax.axis_size("core")
    n_f = n_x * n_c
    t, x, core = lax.axis_index("tensor"), lax.axis_index("x"), lax.axis_index("core")
    tokens, width = resid.shape
    a_rows = MODULES * R // n_f
    rows_dev = 2 * CAND_DEV * a_rows

    module = x % MODULES

    moves = []
    for h in range(n_t):
        for k in range(n_x):
            for c in range(n_c):
                source = (h * n_x + (k + h // n_c) % n_x) * n_c + (c ^ (h % n_c))
                moves.append((source, (h * n_x + k) * n_c + c))
    to_x = (x - t // n_c) % n_x
    wanted = (to_x % MODULES * (n_x // MODULES) + to_x // MODULES) * n_c + (core ^ (t % n_c))
    eigen_part = lax.dynamic_index_in_dim(
        eigenvalues.reshape(n_f, a_rows, width), wanted, axis=0, keepdims=False
    )
    eigen = lax.ppermute(eigen_part, ("tensor", "x", "core"), moves)

    squares, eigen_sums = pl.pallas_call(
        prologue_kernel,
        out_shape=(
            jax.ShapeDtypeStruct((n_t * n_f, tokens // width, width), jnp.float32),
            jax.ShapeDtypeStruct((8, width), jnp.bfloat16),
        ),
        in_specs=[pl.BlockSpec(memory_space=pltpu.VMEM)] * 2,
        out_specs=[pl.BlockSpec(memory_space=pltpu.VMEM)] * 2,
        name="prologue",
    )(resid, eigenvalues)
    squares = lax.all_to_all(squares, ("tensor",) + FACTOR, 0, 0, tiled=True)
    totals = jnp.sum(squares, axis=0).reshape(-1)

    def shifted(value, step):
        return lax.ppermute(value, "x", [((k + step) % n_x, k) for k in range(n_x)])

    across = [shifted(input_basis, step) for step in range(2, n_x, 2)]
    totals, *across = lax.optimization_barrier((totals, *across))
    pick = functools.partial(lax.dynamic_index_in_dim, axis=0, keepdims=False)
    own, rest = pick(input_basis, module), pick(input_basis, 1 - module)
    near = [own] + [
        shifted(rest, step) if step % 2 else pick(across[step // 2 - 1], module)
        for step in range(1, n_x)
    ]
    near = jnp.stack(near)
    far = lax.ppermute(near, "core", [(0, 1), (1, 0)])

    values = resid.astype(jnp.float32)
    normed = (
        values * lax.rsqrt(totals / D + 1e-05)[:, None] * norm_gain.astype(jnp.float32)
    ).astype(jnp.bfloat16)
    onehot = (
        segment_ids[0][None, :] == jnp.arange(CAND_DEV, dtype=jnp.int32)[:, None]
    ).astype(jnp.bfloat16)
    weighted = onehot[:, :, None, None] * cotangent[None]
    grads = jnp.einsum(
        "stmb,ti->smbi", weighted, normed, preferred_element_type=jnp.float32
    ).astype(jnp.bfloat16)
    stack = jnp.concatenate([grads, query_grads], axis=0)
    turned = jnp.einsum(
        "mbxca,nmbi->xmcnai",
        output_basis.reshape(MODULES, R, n_x // MODULES, n_c, a_rows),
        stack,
        preferred_element_type=jnp.float32,
    ).astype(jnp.bfloat16)
    turned = turned.reshape(n_f, rows_dev, width)
    parcel = jnp.concatenate(
        [turned, jnp.broadcast_to(eigen_sums, (n_f,) + eigen_sums.shape)], axis=1
    )
    parcel = jnp.broadcast_to(parcel, (n_dp,) + parcel.shape)
    parcel = parcel.reshape((n_dp * n_f,) + parcel.shape[-2:])
    parcel = lax.all_to_all(parcel, ("dp",) + FACTOR, 0, 0, tiled=True)
    sums = parcel[:, rows_dev : rows_dev + 3 * MODULES].astype(jnp.float32)
    sums = jnp.sum(sums.reshape(-1, MODULES, 3 * width), axis=(0, 2))
    damping = 0.1 * sums / (R * D)

    partial = pl.pallas_call(
        rotate_kernel,
        out_shape=jax.ShapeDtypeStruct((n_t, n_dp * rows_dev, width), jnp.bfloat16),
        in_specs=[pl.BlockSpec(memory_space=pltpu.VMEM)] * 3,
        out_specs=pl.BlockSpec(memory_space=pltpu.VMEM),
        scratch_shapes=[pltpu.VMEM((n_dp * rows_dev, n_f * width), jnp.bfloat16)],
        compiler_params=pltpu.CompilerParams(vmem_limit_bytes=32 << 20),
        name="rotate",
    )(parcel, near, far)
    partial = lax.all_to_all(partial, "tensor", 0, 0, tiled=True)
    rotated = jnp.sum(partial.astype(jnp.float32), axis=0)
    rotated = rotated.reshape(2, n_dp * CAND_DEV, a_rows, width)

    weight = 1.0 / (eigen + lax.dynamic_index_in_dim(damping, module, keepdims=False))
    scores = jnp.einsum(
        "naj,kaj->nk", rotated[0] * weight, rotated[1], precision=lax.Precision.HIGHEST
    )
    shape = scores.shape
    scores = jnp.sum(lax.all_gather(scores.reshape(2, -1), FACTOR, axis=0), axis=0)
    return everywhere(scores, ("dp", "tensor")).reshape(shape)


def solution(mesh):
    n_dp, n_t, n_f = (mesh.shape[name] for name in ("dp", "tensor", "factor"))
    fine = Mesh(mesh.devices.reshape(n_dp, n_t, n_f // 2, 2), ("dp", "tensor") + FACTOR)
    features = ("tensor",) + FACTOR
    columns = ("dp",) + FACTOR
    placed = (
        P("dp", features),
        P(features),
        P("dp", None, None),
        P("dp", None),
        P("dp", None, None, features),
        P(None, "tensor", columns),
        P(),
        P(None, None, columns),
    )
    return jax.shard_map(body, mesh=fine, in_specs=placed, out_specs=P(), check_vma=False)
```

```python
import functools
import math

import jax
import jax.numpy as jnp
from jax import lax
from jax.experimental import pallas as pl
from jax.experimental.pallas import tpu as pltpu
from jax.sharding import Mesh, PartitionSpec as P

D = 8192
R = 64
MODULES = 2
CAND_DEV = 2
FACTOR = ("x", "core")


def everywhere(value, axes):
    peers = math.prod(lax.axis_size(axis) for axis in axes)
    terms = jnp.broadcast_to(value, (peers,) + value.shape)
    return lax.all_to_all(terms, axes, 0, 0, tiled=True)


def prologue_kernel(resid_ref, eigen_ref, squares_ref, sums_ref):
    tokens, width = resid_ref.shape
    rows = []
    for top in range(0, tokens, width):
        values = resid_ref[top : top + width].astype(jnp.float32)
        rows.append(jnp.sum((values * values).T, axis=0, keepdims=True))
    squares_ref[...] = jnp.broadcast_to(jnp.concatenate(rows, axis=0), squares_ref.shape)
    terms = []
    for module in range(MODULES):
        rest = jnp.sum(eigen_ref[module], axis=0, keepdims=True)
        for _ in range(3):
            term = rest.astype(jnp.bfloat16).astype(jnp.float32)
            terms.append(term)
            rest = rest - term
    terms.append(jnp.zeros((sums_ref.shape[0] - 3 * MODULES, width), jnp.float32))
    sums_ref[...] = jnp.concatenate(terms, axis=0).astype(jnp.bfloat16)


def finish_kernel(terms_ref, out_ref):
    total = jnp.sum(terms_ref[...], axis=0)
    size = out_ref.shape[1]
    per_row = total.shape[1] // size
    for row in range(out_ref.shape[0]):
        left = row % per_row * size
        out_ref[row : row + 1, :] = total[row // per_row : row // per_row + 1, left : left + size]


def rotate_kernel(parcel_ref, near_ref, far_ref, out_ref, rows_ref):
    sources, _, width = parcel_ref.shape
    rows, depth = rows_ref.shape
    across = depth // width
    height = rows // 2 // (sources // across)
    for source in range(sources):
        for half in range(2):
            top = half * (rows // 2) + source // across * height
            left = (source % across) * width
            rows_ref[top : top + height, left : left + width] = parcel_ref[
                source, half * height : (half + 1) * height
            ]
    for shift in range(near_ref.shape[0]):
        columns = jnp.concatenate([near_ref[shift], far_ref[shift]], axis=1)
        product = jnp.dot(rows_ref[...], columns, preferred_element_type=jnp.float32)
        out_ref[2 * shift] = product[:, :width].astype(jnp.bfloat16)
        out_ref[2 * shift + 1] = product[:, width:].astype(jnp.bfloat16)


def body(
    resid, norm_gain, cotangent, segment_ids, query_grads, input_basis, output_basis, eigenvalues
):
    n_dp, n_t = lax.axis_size("dp"), lax.axis_size("tensor")
    n_x, n_c = lax.axis_size("x"), lax.axis_size("core")
    n_f = n_x * n_c
    t, x, core = lax.axis_index("tensor"), lax.axis_index("x"), lax.axis_index("core")
    tokens, width = resid.shape
    a_rows = MODULES * R // n_f
    rows_dev = 2 * CAND_DEV * a_rows

    module = x % MODULES

    moves = []
    for h in range(n_t):
        for k in range(n_x):
            for c in range(n_c):
                source = (h * n_x + (k + h // n_c) % n_x) * n_c + (c ^ (h % n_c))
                moves.append((source, (h * n_x + k) * n_c + c))
    to_x = (x - t // n_c) % n_x
    wanted = (to_x % MODULES * (n_x // MODULES) + to_x // MODULES) * n_c + (core ^ (t % n_c))
    eigen_part = lax.dynamic_index_in_dim(
        eigenvalues.reshape(n_f, a_rows, width), wanted, axis=0, keepdims=False
    )
    eigen = lax.ppermute(eigen_part, ("tensor", "x", "core"), moves)

    squares, eigen_sums = pl.pallas_call(
        prologue_kernel,
        out_shape=(
            jax.ShapeDtypeStruct((n_t * n_f, tokens // width, width), jnp.float32),
            jax.ShapeDtypeStruct((8, width), jnp.bfloat16),
        ),
        in_specs=[pl.BlockSpec(memory_space=pltpu.VMEM)] * 2,
        out_specs=[pl.BlockSpec(memory_space=pltpu.VMEM)] * 2,
        name="prologue",
    )(resid, eigenvalues)
    squares = lax.all_to_all(squares, ("tensor",) + FACTOR, 0, 0, tiled=True)
    totals = jnp.sum(squares, axis=0).reshape(-1)

    def shifted(value, step):
        return lax.ppermute(value, "x", [((k + step) % n_x, k) for k in range(n_x)])

    across = [shifted(input_basis, step) for step in range(2, n_x, 2)]
    masked = [
        jnp.where(segment_ids[0] == candidate, cotangent.transpose(1, 2, 0), 0)
        for candidate in range(CAND_DEV)
    ]
    weighted = jnp.stack(masked).reshape(-1, tokens)
    values = resid.astype(jnp.float32)
    totals, weighted, values, *across = lax.optimization_barrier(
        (totals, weighted, values, *across)
    )
    pick = functools.partial(lax.dynamic_index_in_dim, axis=0, keepdims=False)
    own, rest = pick(input_basis, module), pick(input_basis, 1 - module)
    near = [own] + [
        shifted(rest, step) if step % 2 else pick(across[step // 2 - 1], module)
        for step in range(1, n_x)
    ]
    near = jnp.stack(near)
    far = lax.ppermute(near, "core", [(0, 1), (1, 0)])

    normed = (
        values * lax.rsqrt(totals / D + 1e-05)[:, None] * norm_gain.astype(jnp.float32)
    ).astype(jnp.bfloat16)
    grads = jnp.dot(weighted, normed, preferred_element_type=jnp.float32).astype(jnp.bfloat16)
    grads = grads.reshape(CAND_DEV, MODULES, R, width)
    stack = jnp.concatenate([grads, query_grads], axis=0)
    turned = jnp.einsum(
        "mbxca,nmbi->xmcnai",
        output_basis.reshape(MODULES, R, n_x // MODULES, n_c, a_rows),
        stack,
        preferred_element_type=jnp.float32,
    ).astype(jnp.bfloat16)
    turned = turned.reshape(n_f, rows_dev, width)
    parcel = jnp.concatenate(
        [turned, jnp.broadcast_to(eigen_sums, (n_f,) + eigen_sums.shape)], axis=1
    )
    parcel = jnp.broadcast_to(parcel, (n_dp,) + parcel.shape)
    parcel = parcel.reshape((n_dp * n_f,) + parcel.shape[-2:])
    parcel = lax.all_to_all(parcel, ("dp",) + FACTOR, 0, 0, tiled=True)
    sums = parcel[:, rows_dev : rows_dev + 3 * MODULES].astype(jnp.float32)
    sums = jnp.sum(sums.reshape(-1, MODULES, 3 * width), axis=(0, 2))
    damping = 0.1 * sums / (R * D)

    partial = pl.pallas_call(
        rotate_kernel,
        out_shape=jax.ShapeDtypeStruct((n_t, n_dp * rows_dev, width), jnp.bfloat16),
        in_specs=[pl.BlockSpec(memory_space=pltpu.VMEM)] * 3,
        out_specs=pl.BlockSpec(memory_space=pltpu.VMEM),
        scratch_shapes=[pltpu.VMEM((n_dp * rows_dev, n_f * width), jnp.bfloat16)],
        compiler_params=pltpu.CompilerParams(vmem_limit_bytes=32 << 20),
        name="rotate",
    )(parcel, near, far)
    partial = lax.all_to_all(partial, "tensor", 0, 0, tiled=True)
    rotated = jnp.sum(partial.astype(jnp.float32), axis=0)
    rotated = rotated.reshape(2, n_dp * CAND_DEV, a_rows, width)

    weight = 1.0 / (eigen + lax.dynamic_index_in_dim(damping, module, keepdims=False))
    scores = jnp.einsum(
        "naj,kaj->nk", rotated[0] * weight, rotated[1], precision=lax.Precision.HIGHEST
    )
    shape = scores.shape
    scores = jnp.sum(lax.all_gather(scores.reshape(2, -1), FACTOR, axis=0), axis=0)
    return pl.pallas_call(
        finish_kernel,
        out_shape=jax.ShapeDtypeStruct(shape, jnp.float32),
        in_specs=[pl.BlockSpec(memory_space=pltpu.VMEM)],
        out_specs=pl.BlockSpec(memory_space=pltpu.VMEM),
        name="finish",
    )(everywhere(scores, ("dp", "tensor")))


def solution(mesh):
    n_dp, n_t, n_f = (mesh.shape[name] for name in ("dp", "tensor", "factor"))
    fine = Mesh(mesh.devices.reshape(n_dp, n_t, n_f // 2, 2), ("dp", "tensor") + FACTOR)
    features = ("tensor",) + FACTOR
    columns = ("dp",) + FACTOR
    placed = (
        P("dp", features),
        P(features),
        P("dp", None, None),
        P("dp", None),
        P("dp", None, None, features),
        P(None, "tensor", columns),
        P(),
        P(None, None, columns),
    )
    return jax.shard_map(body, mesh=fine, in_specs=placed, out_specs=P(), check_vma=False)
```

```python
import functools
import math

import jax
import jax.numpy as jnp
from jax import lax
from jax.experimental import pallas as pl
from jax.experimental.pallas import tpu as pltpu
from jax.sharding import Mesh, PartitionSpec as P

D = 8192
R = 64
MODULES = 2
CAND_DEV = 2
FACTOR = ("x", "core")


def everywhere(value, axes):
    peers = math.prod(lax.axis_size(axis) for axis in axes)
    terms = jnp.broadcast_to(value, (peers,) + value.shape)
    return lax.all_to_all(terms, axes, 0, 0, tiled=True)


def prologue_kernel(resid_ref, eigen_ref, squares_ref, sums_ref):
    tokens, width = resid_ref.shape
    rows = []
    for top in range(0, tokens, width):
        values = resid_ref[top : top + width].astype(jnp.float32)
        rows.append(jnp.sum((values * values).T, axis=0, keepdims=True))
    squares_ref[...] = jnp.broadcast_to(jnp.concatenate(rows, axis=0), squares_ref.shape)
    terms = []
    for module in range(MODULES):
        rest = jnp.sum(eigen_ref[module], axis=0, keepdims=True)
        for _ in range(3):
            term = rest.astype(jnp.bfloat16).astype(jnp.float32)
            terms.append(term)
            rest = rest - term
    terms.append(jnp.zeros((sums_ref.shape[0] - 3 * MODULES, width), jnp.float32))
    sums_ref[...] = jnp.concatenate(terms, axis=0).astype(jnp.bfloat16)


def rotate_kernel(parcel_ref, near_ref, far_ref, out_ref, rows_ref):
    sources, _, width = parcel_ref.shape
    rows, depth = rows_ref.shape
    across = depth // width
    height = rows // 2 // (sources // across)
    for source in range(sources):
        for half in range(2):
            top = half * (rows // 2) + source // across * height
            left = (source % across) * width
            rows_ref[top : top + height, left : left + width] = parcel_ref[
                source, half * height : (half + 1) * height
            ]
    for shift in range(near_ref.shape[0]):
        columns = jnp.concatenate([near_ref[shift], far_ref[shift]], axis=1)
        product = jnp.dot(rows_ref[...], columns, preferred_element_type=jnp.float32)
        out_ref[2 * shift] = product[:, :width].astype(jnp.bfloat16)
        out_ref[2 * shift + 1] = product[:, width:].astype(jnp.bfloat16)


def body(
    resid, norm_gain, cotangent, segment_ids, query_grads, input_basis, output_basis, eigenvalues
):
    n_dp, n_t = lax.axis_size("dp"), lax.axis_size("tensor")
    n_x, n_c = lax.axis_size("x"), lax.axis_size("core")
    n_f = n_x * n_c
    t, x, core = lax.axis_index("tensor"), lax.axis_index("x"), lax.axis_index("core")
    tokens, width = resid.shape
    a_rows = MODULES * R // n_f
    rows_dev = 2 * CAND_DEV * a_rows

    module = x % MODULES

    moves = []
    for h in range(n_t):
        for k in range(n_x):
            for c in range(n_c):
                source = (h * n_x + (k + h // n_c) % n_x) * n_c + (c ^ (h % n_c))
                moves.append((source, (h * n_x + k) * n_c + c))
    to_x = (x - t // n_c) % n_x
    wanted = (to_x % MODULES * (n_x // MODULES) + to_x // MODULES) * n_c + (core ^ (t % n_c))
    eigen_part = lax.dynamic_index_in_dim(
        eigenvalues.reshape(n_f, a_rows, width), wanted, axis=0, keepdims=False
    )
    eigen = lax.ppermute(eigen_part, ("tensor", "x", "core"), moves)

    squares, eigen_sums = pl.pallas_call(
        prologue_kernel,
        out_shape=(
            jax.ShapeDtypeStruct((n_t * n_f, tokens // width, width), jnp.float32),
            jax.ShapeDtypeStruct((8, width), jnp.bfloat16),
        ),
        in_specs=[pl.BlockSpec(memory_space=pltpu.VMEM)] * 2,
        out_specs=[pl.BlockSpec(memory_space=pltpu.VMEM)] * 2,
        name="prologue",
    )(resid, eigenvalues)
    squares = lax.all_to_all(squares, ("tensor",) + FACTOR, 0, 0, tiled=True)
    totals = jnp.sum(squares, axis=0).reshape(-1)

    def shifted(value, step):
        return lax.ppermute(value, "x", [((k + step) % n_x, k) for k in range(n_x)])

    across = [shifted(input_basis, step) for step in range(2, n_x, 2)]
    masked = [
        jnp.where(segment_ids[0] == candidate, cotangent.transpose(1, 2, 0), 0)
        for candidate in range(CAND_DEV)
    ]
    weighted = jnp.stack(masked).reshape(-1, tokens)
    values = resid.astype(jnp.float32)
    totals, weighted, values, *across = lax.optimization_barrier(
        (totals, weighted, values, *across)
    )
    pick = functools.partial(lax.dynamic_index_in_dim, axis=0, keepdims=False)
    own, rest = pick(input_basis, module), pick(input_basis, 1 - module)
    near = [own] + [
        shifted(rest, step) if step % 2 else pick(across[step // 2 - 1], module)
        for step in range(1, n_x)
    ]
    near = jnp.stack(near)
    far = lax.ppermute(near, "core", [(0, 1), (1, 0)])

    normed = (
        values * lax.rsqrt(totals / D + 1e-05)[:, None] * norm_gain.astype(jnp.float32)
    ).astype(jnp.bfloat16)
    grads = jnp.dot(weighted, normed, preferred_element_type=jnp.float32).astype(jnp.bfloat16)
    grads = grads.reshape(CAND_DEV, MODULES, R, width)
    stack = jnp.concatenate([grads, query_grads], axis=0)
    turned = jnp.einsum(
        "mbxca,nmbi->xmcnai",
        output_basis.reshape(MODULES, R, n_x // MODULES, n_c, a_rows),
        stack,
        preferred_element_type=jnp.float32,
    ).astype(jnp.bfloat16)
    turned = turned.reshape(n_f, rows_dev, width)
    parcel = jnp.concatenate(
        [turned, jnp.broadcast_to(eigen_sums, (n_f,) + eigen_sums.shape)], axis=1
    )
    parcel = jnp.broadcast_to(parcel, (n_dp,) + parcel.shape)
    parcel = parcel.reshape((n_dp * n_f,) + parcel.shape[-2:])
    parcel = lax.all_to_all(parcel, ("dp",) + FACTOR, 0, 0, tiled=True)
    sums = parcel[:, rows_dev : rows_dev + 3 * MODULES].astype(jnp.float32)
    sums = jnp.sum(sums.reshape(-1, MODULES, 3 * width), axis=(0, 2))
    damping = 0.1 * sums / (R * D)

    partial = pl.pallas_call(
        rotate_kernel,
        out_shape=jax.ShapeDtypeStruct((n_t, n_dp * rows_dev, width), jnp.bfloat16),
        in_specs=[pl.BlockSpec(memory_space=pltpu.VMEM)] * 3,
        out_specs=pl.BlockSpec(memory_space=pltpu.VMEM),
        scratch_shapes=[pltpu.VMEM((n_dp * rows_dev, n_f * width), jnp.bfloat16)],
        compiler_params=pltpu.CompilerParams(vmem_limit_bytes=32 << 20),
        name="rotate",
    )(parcel, near, far)
    partial = lax.all_to_all(partial, "tensor", 0, 0, tiled=True)
    rotated = jnp.sum(partial.astype(jnp.float32), axis=0)
    rotated = rotated.reshape(2, n_dp * CAND_DEV, a_rows, width)

    weight = 1.0 / (eigen + lax.dynamic_index_in_dim(damping, module, keepdims=False))
    scores = jnp.einsum(
        "naj,kaj->nk", rotated[0] * weight, rotated[1], precision=lax.Precision.HIGHEST
    )
    shape = scores.shape
    scores = jnp.sum(lax.all_gather(scores.reshape(2, -1), FACTOR, axis=0), axis=0)
    return jnp.sum(everywhere(scores, ("dp", "tensor")), axis=0).reshape(shape)


def solution(mesh):
    n_dp, n_t, n_f = (mesh.shape[name] for name in ("dp", "tensor", "factor"))
    fine = Mesh(mesh.devices.reshape(n_dp, n_t, n_f // 2, 2), ("dp", "tensor") + FACTOR)
    features = ("tensor",) + FACTOR
    columns = ("dp",) + FACTOR
    placed = (
        P("dp", features),
        P(features),
        P("dp", None, None),
        P("dp", None),
        P("dp", None, None, features),
        P(None, "tensor", columns),
        P(),
        P(None, None, columns),
    )
    return jax.shard_map(body, mesh=fine, in_specs=placed, out_specs=P(), check_vma=False)
```

```python
import functools
import math

import jax
import jax.numpy as jnp
from jax import lax
from jax.experimental import pallas as pl
from jax.experimental.pallas import tpu as pltpu
from jax.sharding import Mesh, PartitionSpec as P

D = 8192
R = 64
MODULES = 2
CAND_DEV = 2
FACTOR = ("x", "core")


def everywhere(value, axes):
    peers = math.prod(lax.axis_size(axis) for axis in axes)
    terms = jnp.broadcast_to(value, (peers,) + value.shape)
    return lax.all_to_all(terms, axes, 0, 0, tiled=True)


def prologue_kernel(resid_ref, eigen_ref, squares_ref, sums_ref):
    tokens, width = resid_ref.shape
    rows = []
    for top in range(0, tokens, width):
        values = resid_ref[top : top + width].astype(jnp.float32)
        rows.append(jnp.sum((values * values).T, axis=0, keepdims=True))
    squares_ref[...] = jnp.broadcast_to(jnp.concatenate(rows, axis=0), squares_ref.shape)
    terms = []
    for module in range(MODULES):
        rest = jnp.sum(eigen_ref[module], axis=0, keepdims=True)
        for _ in range(3):
            term = rest.astype(jnp.bfloat16).astype(jnp.float32)
            terms.append(term)
            rest = rest - term
    terms.append(jnp.zeros((sums_ref.shape[0] - 3 * MODULES, width), jnp.float32))
    sums_ref[...] = jnp.concatenate(terms, axis=0).astype(jnp.bfloat16)


def rotate_kernel(parcel_ref, near_ref, far_ref, out_ref, rows_ref):
    sources, _, width = parcel_ref.shape
    rows, depth = rows_ref.shape
    across = depth // width
    height = rows // 2 // (sources // across)
    for source in range(sources):
        for half in range(2):
            top = half * (rows // 2) + source // across * height
            left = (source % across) * width
            rows_ref[top : top + height, left : left + width] = parcel_ref[
                source, half * height : (half + 1) * height
            ]
    for shift in range(near_ref.shape[0]):
        columns = jnp.concatenate([near_ref[shift], far_ref[shift]], axis=1)
        product = jnp.dot(rows_ref[...], columns, preferred_element_type=jnp.float32)
        out_ref[2 * shift] = product[:, :width].astype(jnp.bfloat16)
        out_ref[2 * shift + 1] = product[:, width:].astype(jnp.bfloat16)


def body(
    resid, norm_gain, cotangent, segment_ids, query_grads, input_basis, output_basis, eigenvalues
):
    n_dp, n_t = lax.axis_size("dp"), lax.axis_size("tensor")
    n_x, n_c = lax.axis_size("x"), lax.axis_size("core")
    n_f = n_x * n_c
    t, x, core = lax.axis_index("tensor"), lax.axis_index("x"), lax.axis_index("core")
    tokens, width = resid.shape
    a_rows = MODULES * R // n_f
    rows_dev = 2 * CAND_DEV * a_rows

    module = x % MODULES

    moves = []
    for h in range(n_t):
        for k in range(n_x):
            for c in range(n_c):
                source = (h * n_x + (k + h // n_c) % n_x) * n_c + (c ^ (h % n_c))
                moves.append((source, (h * n_x + k) * n_c + c))
    to_x = (x - t // n_c) % n_x
    wanted = (to_x % MODULES * (n_x // MODULES) + to_x // MODULES) * n_c + (core ^ (t % n_c))
    eigen_part = lax.dynamic_index_in_dim(
        eigenvalues.reshape(n_f, a_rows, width), wanted, axis=0, keepdims=False
    )
    eigen = lax.ppermute(eigen_part, ("tensor", "x", "core"), moves)

    squares, eigen_sums = pl.pallas_call(
        prologue_kernel,
        out_shape=(
            jax.ShapeDtypeStruct((n_t * n_f, tokens // width, width), jnp.float32),
            jax.ShapeDtypeStruct((8, width), jnp.bfloat16),
        ),
        in_specs=[pl.BlockSpec(memory_space=pltpu.VMEM)] * 2,
        out_specs=[pl.BlockSpec(memory_space=pltpu.VMEM)] * 2,
        name="prologue",
    )(resid, eigenvalues)
    squares = lax.all_to_all(squares, ("tensor",) + FACTOR, 0, 0, tiled=True)
    totals = jnp.sum(squares, axis=0).reshape(-1)

    def shifted(value, step):
        return lax.ppermute(value, "x", [((k + step) % n_x, k) for k in range(n_x)])

    across = [shifted(input_basis, step) for step in range(2, n_x, 2)]
    masked = [
        jnp.where(segment_ids[0] == candidate, cotangent.transpose(1, 2, 0), 0)
        for candidate in range(CAND_DEV)
    ]
    weighted = jnp.stack(masked).reshape(-1, tokens)
    values = resid.astype(jnp.float32)
    totals, weighted, values = lax.optimization_barrier((totals, weighted, values))
    pick = functools.partial(lax.dynamic_index_in_dim, axis=0, keepdims=False)
    own, rest = pick(input_basis, module), pick(input_basis, 1 - module)
    near = [own] + [
        shifted(rest, step) if step % 2 else pick(across[step // 2 - 1], module)
        for step in range(1, n_x)
    ]
    near = jnp.stack(near)
    far = lax.ppermute(near, "core", [(0, 1), (1, 0)])

    normed = (
        values * lax.rsqrt(totals / D + 1e-05)[:, None] * norm_gain.astype(jnp.float32)
    ).astype(jnp.bfloat16)
    grads = jnp.dot(weighted, normed, preferred_element_type=jnp.float32).astype(jnp.bfloat16)
    grads = grads.reshape(CAND_DEV, MODULES, R, width)
    stack = jnp.concatenate([grads, query_grads], axis=0)
    turned = jnp.einsum(
        "mbxca,nmbi->xmcnai",
        output_basis.reshape(MODULES, R, n_x // MODULES, n_c, a_rows),
        stack,
        preferred_element_type=jnp.float32,
    ).astype(jnp.bfloat16)
    turned = turned.reshape(n_f, rows_dev, width)
    parcel = jnp.concatenate(
        [turned, jnp.broadcast_to(eigen_sums, (n_f,) + eigen_sums.shape)], axis=1
    )
    parcel = jnp.broadcast_to(parcel, (n_dp,) + parcel.shape)
    parcel = parcel.reshape((n_dp * n_f,) + parcel.shape[-2:])
    parcel, *across = lax.optimization_barrier((parcel, *across))
    parcel = lax.all_to_all(parcel, ("dp",) + FACTOR, 0, 0, tiled=True)
    sums = parcel[:, rows_dev : rows_dev + 3 * MODULES].astype(jnp.float32)
    sums = jnp.sum(sums.reshape(-1, MODULES, 3 * width), axis=(0, 2))
    damping = 0.1 * sums / (R * D)

    partial = pl.pallas_call(
        rotate_kernel,
        out_shape=jax.ShapeDtypeStruct((n_t, n_dp * rows_dev, width), jnp.bfloat16),
        in_specs=[pl.BlockSpec(memory_space=pltpu.VMEM)] * 3,
        out_specs=pl.BlockSpec(memory_space=pltpu.VMEM),
        scratch_shapes=[pltpu.VMEM((n_dp * rows_dev, n_f * width), jnp.bfloat16)],
        compiler_params=pltpu.CompilerParams(vmem_limit_bytes=32 << 20),
        name="rotate",
    )(parcel, near, far)
    partial = lax.all_to_all(partial, "tensor", 0, 0, tiled=True)
    rotated = jnp.sum(partial.astype(jnp.float32), axis=0)
    rotated = rotated.reshape(2, n_dp * CAND_DEV, a_rows, width)

    weight = 1.0 / (eigen + lax.dynamic_index_in_dim(damping, module, keepdims=False))
    scores = jnp.einsum(
        "naj,kaj->nk", rotated[0] * weight, rotated[1], precision=lax.Precision.HIGHEST
    )
    shape = scores.shape
    scores = jnp.sum(lax.all_gather(scores.reshape(2, -1), FACTOR, axis=0), axis=0)
    return jnp.sum(everywhere(scores, ("dp", "tensor")), axis=0).reshape(shape)


def solution(mesh):
    n_dp, n_t, n_f = (mesh.shape[name] for name in ("dp", "tensor", "factor"))
    fine = Mesh(mesh.devices.reshape(n_dp, n_t, n_f // 2, 2), ("dp", "tensor") + FACTOR)
    features = ("tensor",) + FACTOR
    columns = ("dp",) + FACTOR
    placed = (
        P("dp", features),
        P(features),
        P("dp", None, None),
        P("dp", None),
        P("dp", None, None, features),
        P(None, "tensor", columns),
        P(),
        P(None, None, columns),
    )
    return jax.shard_map(body, mesh=fine, in_specs=placed, out_specs=P(), check_vma=False)
```

```python
import functools
import math

import jax
import jax.numpy as jnp
from jax import lax
from jax.experimental import pallas as pl
from jax.experimental.pallas import tpu as pltpu
from jax.sharding import Mesh, PartitionSpec as P

D = 8192
R = 64
MODULES = 2
CAND_DEV = 2
FACTOR = ("x", "core")


def everywhere(value, axes):
    peers = math.prod(lax.axis_size(axis) for axis in axes)
    terms = jnp.broadcast_to(value, (peers,) + value.shape)
    return lax.all_to_all(terms, axes, 0, 0, tiled=True)


def prologue_kernel(resid_ref, eigen_ref, squares_ref, sums_ref):
    tokens, width = resid_ref.shape
    rows = []
    for top in range(0, tokens, width):
        values = resid_ref[top : top + width].astype(jnp.float32)
        rows.append(jnp.sum((values * values).T, axis=0, keepdims=True))
    squares_ref[...] = jnp.broadcast_to(jnp.concatenate(rows, axis=0), squares_ref.shape)
    terms = []
    for module in range(MODULES):
        rest = jnp.sum(eigen_ref[module], axis=0, keepdims=True)
        for _ in range(3):
            term = rest.astype(jnp.bfloat16).astype(jnp.float32)
            terms.append(term)
            rest = rest - term
    terms.append(jnp.zeros((sums_ref.shape[0] - 3 * MODULES, width), jnp.float32))
    sums_ref[...] = jnp.concatenate(terms, axis=0).astype(jnp.bfloat16)


def rotate_kernel(parcel_ref, near_ref, far_ref, out_ref, rows_ref, part_ref, sems):
    sources, _, width = parcel_ref.shape
    rows, depth = rows_ref.shape
    across = depth // width
    height = rows // 2 // (sources // across)
    for source in range(sources):
        for half in range(2):
            top = half * (rows // 2) + source // across * height
            left = (source % across) * width
            rows_ref[top : top + height, left : left + width] = parcel_ref[
                source, half * height : (half + 1) * height
            ]
    copies = []
    for shift in range(near_ref.shape[0]):
        columns = jnp.concatenate([near_ref[shift], far_ref[shift]], axis=1)
        product = jnp.dot(rows_ref[...], columns, preferred_element_type=jnp.float32)
        part_ref[shift, 0] = product[:, :width].astype(jnp.bfloat16)
        part_ref[shift, 1] = product[:, width:].astype(jnp.bfloat16)
        copy = pltpu.make_async_copy(part_ref.at[shift], out_ref.at[shift], sems.at[shift])
        copy.start()
        copies.append(copy)
    for copy in copies:
        copy.wait()


def body(
    resid, norm_gain, cotangent, segment_ids, query_grads, input_basis, output_basis, eigenvalues
):
    n_dp, n_t = lax.axis_size("dp"), lax.axis_size("tensor")
    n_x, n_c = lax.axis_size("x"), lax.axis_size("core")
    n_f = n_x * n_c
    t, x, core = lax.axis_index("tensor"), lax.axis_index("x"), lax.axis_index("core")
    tokens, width = resid.shape
    a_rows = MODULES * R // n_f
    rows_dev = 2 * CAND_DEV * a_rows

    module = x % MODULES

    moves = []
    for h in range(n_t):
        for k in range(n_x):
            for c in range(n_c):
                source = (h * n_x + (k + h // n_c) % n_x) * n_c + (c ^ (h % n_c))
                moves.append((source, (h * n_x + k) * n_c + c))
    to_x = (x - t // n_c) % n_x
    wanted = (to_x % MODULES * (n_x // MODULES) + to_x // MODULES) * n_c + (core ^ (t % n_c))
    eigen_part = lax.dynamic_index_in_dim(
        eigenvalues.reshape(n_f, a_rows, width), wanted, axis=0, keepdims=False
    )
    eigen = lax.ppermute(eigen_part, ("tensor", "x", "core"), moves)

    squares, eigen_sums = pl.pallas_call(
        prologue_kernel,
        out_shape=(
            jax.ShapeDtypeStruct((n_t * n_f, tokens // width, width), jnp.float32),
            jax.ShapeDtypeStruct((8, width), jnp.bfloat16),
        ),
        in_specs=[pl.BlockSpec(memory_space=pltpu.VMEM)] * 2,
        out_specs=[pl.BlockSpec(memory_space=pltpu.VMEM)] * 2,
        name="prologue",
    )(resid, eigenvalues)
    squares = lax.all_to_all(squares, ("tensor",) + FACTOR, 0, 0, tiled=True)
    totals = jnp.sum(squares, axis=0).reshape(-1)

    def shifted(value, step):
        return lax.ppermute(value, "x", [((k + step) % n_x, k) for k in range(n_x)])

    across = [shifted(input_basis, step) for step in range(2, n_x, 2)]
    masked = [
        jnp.where(segment_ids[0] == candidate, cotangent.transpose(1, 2, 0), 0)
        for candidate in range(CAND_DEV)
    ]
    weighted = jnp.stack(masked).reshape(-1, tokens)
    values = resid.astype(jnp.float32)
    totals, weighted, values, *across = lax.optimization_barrier(
        (totals, weighted, values, *across)
    )
    pick = functools.partial(lax.dynamic_index_in_dim, axis=0, keepdims=False)
    own, rest = pick(input_basis, module), pick(input_basis, 1 - module)
    near = [own] + [
        shifted(rest, step) if step % 2 else pick(across[step // 2 - 1], module)
        for step in range(1, n_x)
    ]
    near = jnp.stack(near)
    far = lax.ppermute(near, "core", [(0, 1), (1, 0)])

    normed = (
        values * lax.rsqrt(totals / D + 1e-05)[:, None] * norm_gain.astype(jnp.float32)
    ).astype(jnp.bfloat16)
    grads = jnp.dot(weighted, normed, preferred_element_type=jnp.float32).astype(jnp.bfloat16)
    grads = grads.reshape(CAND_DEV, MODULES, R, width)
    stack = jnp.concatenate([grads, query_grads], axis=0)
    turned = jnp.einsum(
        "mbxca,nmbi->xmcnai",
        output_basis.reshape(MODULES, R, n_x // MODULES, n_c, a_rows),
        stack,
        preferred_element_type=jnp.float32,
    ).astype(jnp.bfloat16)
    turned = turned.reshape(n_f, rows_dev, width)
    parcel = jnp.concatenate(
        [turned, jnp.broadcast_to(eigen_sums, (n_f,) + eigen_sums.shape)], axis=1
    )
    parcel = jnp.broadcast_to(parcel, (n_dp,) + parcel.shape)
    parcel = parcel.reshape((n_dp * n_f,) + parcel.shape[-2:])
    parcel = lax.all_to_all(parcel, ("dp",) + FACTOR, 0, 0, tiled=True)
    sums = parcel[:, rows_dev : rows_dev + 3 * MODULES].astype(jnp.float32)
    sums = jnp.sum(sums.reshape(-1, MODULES, 3 * width), axis=(0, 2))
    damping = 0.1 * sums / (R * D)

    shape = (n_x, n_c, n_dp * rows_dev, width)
    partial = pl.pallas_call(
        rotate_kernel,
        out_shape=jax.ShapeDtypeStruct(shape, jnp.bfloat16),
        in_specs=[pl.BlockSpec(memory_space=pltpu.VMEM)] * 3,
        out_specs=pl.BlockSpec(memory_space=pl.ANY),
        scratch_shapes=[
            pltpu.VMEM((n_dp * rows_dev, n_f * width), jnp.bfloat16),
            pltpu.VMEM(shape, jnp.bfloat16),
            pltpu.SemaphoreType.DMA((n_x,)),
        ],
        compiler_params=pltpu.CompilerParams(vmem_limit_bytes=32 << 20),
        name="rotate",
    )(parcel, near, far)
    partial = partial.reshape((n_t,) + shape[2:])
    partial = lax.all_to_all(partial, "tensor", 0, 0, tiled=True)
    rotated = jnp.sum(partial.astype(jnp.float32), axis=0)
    rotated = rotated.reshape(2, n_dp * CAND_DEV, a_rows, width)

    weight = 1.0 / (eigen + lax.dynamic_index_in_dim(damping, module, keepdims=False))
    scores = jnp.einsum(
        "naj,kaj->nk", rotated[0] * weight, rotated[1], precision=lax.Precision.HIGHEST
    )
    shape = scores.shape
    scores = jnp.sum(lax.all_gather(scores.reshape(2, -1), FACTOR, axis=0), axis=0)
    return jnp.sum(everywhere(scores, ("dp", "tensor")), axis=0).reshape(shape)


def solution(mesh):
    n_dp, n_t, n_f = (mesh.shape[name] for name in ("dp", "tensor", "factor"))
    fine = Mesh(mesh.devices.reshape(n_dp, n_t, n_f // 2, 2), ("dp", "tensor") + FACTOR)
    features = ("tensor",) + FACTOR
    columns = ("dp",) + FACTOR
    placed = (
        P("dp", features),
        P(features),
        P("dp", None, None),
        P("dp", None),
        P("dp", None, None, features),
        P(None, "tensor", columns),
        P(),
        P(None, None, columns),
    )
    return jax.shard_map(body, mesh=fine, in_specs=placed, out_specs=P(), check_vma=False)
```

```python
import functools
import math

import jax
import jax.numpy as jnp
from jax import lax
from jax.experimental import pallas as pl
from jax.experimental.pallas import tpu as pltpu
from jax.sharding import Mesh, PartitionSpec as P

D = 8192
R = 64
MODULES = 2
CAND_DEV = 2
FACTOR = ("x", "core")


def everywhere(value, axes):
    peers = math.prod(lax.axis_size(axis) for axis in axes)
    terms = jnp.broadcast_to(value, (peers,) + value.shape)
    return lax.all_to_all(terms, axes, 0, 0, tiled=True)


def prologue_kernel(resid_ref, eigen_ref, squares_ref, sums_ref):
    tokens, width = resid_ref.shape
    rows = []
    for top in range(0, tokens, width):
        values = resid_ref[top : top + width].astype(jnp.float32)
        rows.append(jnp.sum((values * values).T, axis=0, keepdims=True))
    squares_ref[...] = jnp.broadcast_to(jnp.concatenate(rows, axis=0), squares_ref.shape)
    terms = []
    for module in range(MODULES):
        rest = jnp.sum(eigen_ref[module], axis=0, keepdims=True)
        for _ in range(3):
            term = rest.astype(jnp.bfloat16).astype(jnp.float32)
            terms.append(term)
            rest = rest - term
    terms.append(jnp.zeros((sums_ref.shape[0] - 3 * MODULES, width), jnp.float32))
    sums_ref[...] = jnp.concatenate(terms, axis=0).astype(jnp.bfloat16)


def rotate_kernel(parcel_ref, near_ref, far_ref, out_ref, rows_ref, part_ref, sems):
    sources, _, width = parcel_ref.shape
    rows, depth = rows_ref.shape
    across = depth // width
    height = rows // 2 // (sources // across)
    for source in range(sources):
        for half in range(2):
            top = half * (rows // 2) + source // across * height
            left = (source % across) * width
            rows_ref[top : top + height, left : left + width] = parcel_ref[
                source, half * height : (half + 1) * height
            ]
    copies = []
    for shift in range(near_ref.shape[0]):
        columns = jnp.concatenate([near_ref[shift], far_ref[shift]], axis=1)
        product = jnp.dot(rows_ref[...], columns, preferred_element_type=jnp.float32)
        part_ref[shift, 0] = product[:, :width].astype(jnp.bfloat16)
        part_ref[shift, 1] = product[:, width:].astype(jnp.bfloat16)
        copy = pltpu.make_async_copy(part_ref.at[shift], out_ref.at[shift], sems.at[shift])
        copy.start()
        copies.append(copy)
    for copy in copies:
        copy.wait()


def body(
    resid, norm_gain, cotangent, segment_ids, query_grads, input_basis, output_basis, eigenvalues
):
    n_dp, n_t = lax.axis_size("dp"), lax.axis_size("tensor")
    n_x, n_c = lax.axis_size("x"), lax.axis_size("core")
    n_f = n_x * n_c
    t, x, core = lax.axis_index("tensor"), lax.axis_index("x"), lax.axis_index("core")
    tokens, width = resid.shape
    a_rows = MODULES * R // n_f
    rows_dev = 2 * CAND_DEV * a_rows

    module = x % MODULES

    moves = []
    for h in range(n_t):
        for k in range(n_x):
            for c in range(n_c):
                source = (h * n_x + (k + h // n_c) % n_x) * n_c + (c ^ (h % n_c))
                moves.append((source, (h * n_x + k) * n_c + c))
    to_x = (x - t // n_c) % n_x
    wanted = (to_x % MODULES * (n_x // MODULES) + to_x // MODULES) * n_c + (core ^ (t % n_c))
    eigen_part = lax.dynamic_index_in_dim(
        eigenvalues.reshape(n_f, a_rows, width), wanted, axis=0, keepdims=False
    )
    eigen = lax.ppermute(eigen_part, ("tensor", "x", "core"), moves)

    squares, eigen_sums = pl.pallas_call(
        prologue_kernel,
        out_shape=(
            jax.ShapeDtypeStruct((n_t * n_f, tokens // width, width), jnp.float32),
            jax.ShapeDtypeStruct((8, width), jnp.bfloat16),
        ),
        in_specs=[pl.BlockSpec(memory_space=pltpu.VMEM)] * 2,
        out_specs=[pl.BlockSpec(memory_space=pltpu.VMEM)] * 2,
        name="prologue",
    )(resid, eigenvalues)
    squares = lax.all_to_all(squares, FACTOR + ("tensor",), 0, 0, tiled=True)
    totals = jnp.sum(squares, axis=0).reshape(-1)

    def shifted(value, step):
        return lax.ppermute(value, "x", [((k + step) % n_x, k) for k in range(n_x)])

    across = [shifted(input_basis, step) for step in range(2, n_x, 2)]
    masked = [
        jnp.where(segment_ids[0] == candidate, cotangent.transpose(1, 2, 0), 0)
        for candidate in range(CAND_DEV)
    ]
    weighted = jnp.stack(masked).reshape(-1, tokens)
    values = resid.astype(jnp.float32)
    totals, weighted, values, *across = lax.optimization_barrier(
        (totals, weighted, values, *across)
    )
    pick = functools.partial(lax.dynamic_index_in_dim, axis=0, keepdims=False)
    own, rest = pick(input_basis, module), pick(input_basis, 1 - module)
    near = [own] + [
        shifted(rest, step) if step % 2 else pick(across[step // 2 - 1], module)
        for step in range(1, n_x)
    ]
    near = jnp.stack(near)
    far = lax.ppermute(near, "core", [(0, 1), (1, 0)])

    normed = (
        values * lax.rsqrt(totals / D + 1e-05)[:, None] * norm_gain.astype(jnp.float32)
    ).astype(jnp.bfloat16)
    grads = jnp.dot(weighted, normed, preferred_element_type=jnp.float32).astype(jnp.bfloat16)
    grads = grads.reshape(CAND_DEV, MODULES, R, width)
    stack = jnp.concatenate([grads, query_grads], axis=0)
    turned = jnp.einsum(
        "mbxca,nmbi->xmcnai",
        output_basis.reshape(MODULES, R, n_x // MODULES, n_c, a_rows),
        stack,
        preferred_element_type=jnp.float32,
    ).astype(jnp.bfloat16)
    turned = turned.reshape(n_f, rows_dev, width)
    parcel = jnp.concatenate(
        [turned, jnp.broadcast_to(eigen_sums, (n_f,) + eigen_sums.shape)], axis=1
    )
    parcel = jnp.broadcast_to(parcel, (n_dp,) + parcel.shape)
    parcel = parcel.reshape((n_dp * n_f,) + parcel.shape[-2:])
    parcel = lax.all_to_all(parcel, ("dp",) + FACTOR, 0, 0, tiled=True)
    sums = parcel[:, rows_dev : rows_dev + 3 * MODULES].astype(jnp.float32)
    sums = jnp.sum(sums.reshape(-1, MODULES, 3 * width), axis=(0, 2))
    damping = 0.1 * sums / (R * D)

    shape = (n_x, n_c, n_dp * rows_dev, width)
    partial = pl.pallas_call(
        rotate_kernel,
        out_shape=jax.ShapeDtypeStruct(shape, jnp.bfloat16),
        in_specs=[pl.BlockSpec(memory_space=pltpu.VMEM)] * 3,
        out_specs=pl.BlockSpec(memory_space=pl.ANY),
        scratch_shapes=[
            pltpu.VMEM((n_dp * rows_dev, n_f * width), jnp.bfloat16),
            pltpu.VMEM(shape, jnp.bfloat16),
            pltpu.SemaphoreType.DMA((n_x,)),
        ],
        compiler_params=pltpu.CompilerParams(vmem_limit_bytes=32 << 20),
        name="rotate",
    )(parcel, near, far)
    partial = partial.reshape((n_t,) + shape[2:])
    partial = lax.all_to_all(partial, "tensor", 0, 0, tiled=True)
    rotated = jnp.sum(partial.astype(jnp.float32), axis=0)
    rotated = rotated.reshape(2, n_dp * CAND_DEV, a_rows, width)

    weight = 1.0 / (eigen + lax.dynamic_index_in_dim(damping, module, keepdims=False))
    scores = jnp.einsum(
        "naj,kaj->nk", rotated[0] * weight, rotated[1], precision=lax.Precision.HIGHEST
    )
    shape = scores.shape
    scores = jnp.sum(lax.all_gather(scores.reshape(2, -1), FACTOR, axis=0), axis=0)
    return jnp.sum(everywhere(scores, ("tensor", "dp")), axis=0).reshape(shape)


def solution(mesh):
    n_dp, n_t, n_f = (mesh.shape[name] for name in ("dp", "tensor", "factor"))
    fine = Mesh(mesh.devices.reshape(n_dp, n_t, n_f // 2, 2), ("dp", "tensor") + FACTOR)
    features = ("tensor",) + FACTOR
    columns = ("dp",) + FACTOR
    placed = (
        P("dp", features),
        P(features),
        P("dp", None, None),
        P("dp", None),
        P("dp", None, None, features),
        P(None, "tensor", columns),
        P(),
        P(None, None, columns),
    )
    return jax.shard_map(body, mesh=fine, in_specs=placed, out_specs=P(), check_vma=False)
```
